512 devices in a mesh: ia: 8 (over x, z_hi), ja: 8 (over y), ka: 8 (over z_lo, core).
Axes of the slice: x: 4, y: 8, z: 8 (z_hi: 2, z_lo: 4; z = z_hi * 4 + z_lo), core: 2. Of those that a mesh axis runs over, the one named last changes fastest.
Arguments:
- pair_rep: float32 [1024, 1024, 128], P('ia', ('ja', 'ka')), may hold values from -6 to 6
- pair_proj: bfloat16 [128, 512], replicated, may hold values from -0.5 to 0.5
- gate_proj: bfloat16 [128, 128], replicated, may hold values from -0.5 to 0.5
- out_proj: bfloat16 [128, 128], replicated, may hold values from -0.5 to 0.5
- trans_in: bfloat16 [128, 1024], replicated, may hold values from -0.5 to 0.5
- trans_out: bfloat16 [512, 128], replicated, may hold values from -0.25 to 0.25
Outputs:
- pair_out: float32 [1024, 1024, 128], P('ia', ('ja', 'ka'))
The draws below stay inside these ranges and needn't reach their ends.
All inputs are finite; a program needn't handle non-finite values.
Results may differ from the reference program's by a relative error of at most 0.013.
Values may be sent and summed in bfloat16 or wider, within the bound.
No kernel may reach another device: no remote copies, remote signals or barrier semaphores. Data moves between devices by JAX's collectives and lax.ppermute only.
A program may use at most 64 MiB of HBM per device.

```python
import jax
import jax.numpy as jnp
from jax import lax

C = 128
HID = 128
TR = 512
N = 1024
COLW = 16
N_IA = 8
N_JA = 8
N_KA = 8


def shard_levels(own_key, dims, pieces, low, top_value):
    factor_of, own = 1.0, jax.random.fold_in(own_key, 6)
    for dim, shards_of in pieces:
        heights = jnp.exp(jax.random.uniform(jax.random.fold_in(own, dim), (shards_of,), jnp.float32, low / len(pieces), top_value / len(pieces)))
        factor_of = factor_of * jnp.repeat(heights, dims[dim] // shards_of).reshape([-1 if axis == dim else 1 for axis in range(len(dims))])
    return factor_of


def bell_draw(key, extent, width, most, cuts=(), dtype=jnp.bfloat16):
    array = jax.random.normal(key, extent, jnp.float32) * width
    if len(cuts) > 0:
        array = shard_levels(key, extent, cuts, -0.22, 0.18) * array
    return jnp.clip(array, min=-most, max=most).astype(dtype)


def setup_inputs(seed: int = 0) -> dict:
    arg_keys = jax.random.split(jax.random.key(seed), 7)
    pair_rep = bell_draw(arg_keys[0], (N, N, C), 1.0, 6.0, ((0, 8), (1, 64)), jnp.float32)
    pair_proj = bell_draw(arg_keys[1], (C, 4 * HID), C ** -0.5, 0.5)
    gate_proj = bell_draw(arg_keys[2], (C, C), C ** -0.5, 0.5)
    out_proj = bell_draw(arg_keys[3], (HID, C), HID ** -0.5, 0.5)
    trans_in = bell_draw(arg_keys[4], (C, 2 * TR), C ** -0.5, 0.5)
    trans_out = bell_draw(arg_keys[5], (TR, C), TR ** -0.5, 0.25)
    return {"pair_rep": pair_rep, "pair_proj": pair_proj, "gate_proj": gate_proj, "out_proj": out_proj, "trans_in": trans_in, "trans_out": trans_out}


def layer_norm(values):
    centre = lax.optimization_barrier(jnp.mean(values, axis=-1, keepdims=True))
    centred = values - centre
    spread = lax.optimization_barrier(jnp.mean(centred * centred, axis=-1, keepdims=True))
    return centred * lax.rsqrt(spread + 1e-05)

def reference(pair_rep, pair_proj, gate_proj, out_proj, trans_in, trans_out):
    slabs = pair_rep.reshape(N_IA, N // N_IA, N, C)

    def left_right(slab):
        normed = layer_norm(slab).astype(jnp.bfloat16)
        projected = jnp.dot(normed, pair_proj, preferred_element_type=jnp.float32)
        left = (jax.nn.sigmoid(projected[..., :HID]) * projected[..., HID:2 * HID]).astype(jnp.bfloat16)
        right = (jax.nn.sigmoid(projected[..., 2 * HID:3 * HID]) * projected[..., 3 * HID:]).astype(jnp.bfloat16)
        return (left, right)
    left, right = lax.map(left_right, slabs)
    left = left.reshape(N, N_JA, N_KA, COLW, HID)
    right = right.reshape(N, N_JA, N_KA, COLW, HID)
    running = jnp.zeros((N, N, HID), jnp.float32)
    for kblock in range(N_KA):
        left_set = left[:, :, kblock].reshape(N, N_JA * COLW, HID).astype(jnp.float32)
        right_set = right[:, :, kblock].reshape(N, N_JA * COLW, HID).astype(jnp.float32)
        partial_value = jnp.einsum('ikc,jkc->ijc', left_set, right_set).astype(jnp.bfloat16)
        partial_value = lax.optimization_barrier(partial_value)
        running = running + partial_value.astype(jnp.float32)
    tri_slabs = running.reshape(N_IA, N // N_IA, N, HID)

    def finish(inputs):
        slab, tri_slab = inputs
        normed = layer_norm(slab).astype(jnp.bfloat16)
        gating = jax.nn.sigmoid(jnp.dot(normed, gate_proj, preferred_element_type=jnp.float32))
        tri_normed = layer_norm(tri_slab).astype(jnp.bfloat16)
        middle = slab + gating * jnp.dot(tri_normed, out_proj, preferred_element_type=jnp.float32)
        mid_normed = layer_norm(middle).astype(jnp.bfloat16)
        expanded = jnp.dot(mid_normed, trans_in, preferred_element_type=jnp.float32)
        hidden_units = (jax.nn.silu(expanded[..., :TR]) * expanded[..., TR:]).astype(jnp.bfloat16)
        return middle + jnp.dot(hidden_units, trans_out, preferred_element_type=jnp.float32)
    result = lax.map(finish, (slabs, tri_slabs))
    return result.reshape(N, N, C)
```

```python
import functools

import jax
import jax.numpy as jnp
from jax import lax
from jax.experimental import pallas as pl
from jax.experimental.pallas import tpu as pltpu
from jax.sharding import Mesh
from jax.sharding import PartitionSpec as P

AXES = ("xh", "xb", "zh", "y", "zl", "core")
SIZES = (2, 2, 2, 8, 4, 2)
PLANE = ("xh", "zh", "y", "zl")
QUAD = ("xb", "core")
ROWS = 128
COLS = 16
CH = 128
EPS = 1e-05
LIMIT = 56 * 1024 * 1024


def sigmoid(v):
    return 0.5 * jnp.tanh(0.5 * v) + 0.5


def norm_lanes(v):
    centred = v - jnp.mean(v, axis=1, keepdims=True)
    spread = jnp.mean(centred * centred, axis=1, keepdims=True)
    return (centred * lax.rsqrt(spread + EPS)).astype(jnp.bfloat16)


def contract(a, b, dim_a, dim_b):
    return lax.dot_general(a, b, (((dim_a,), (dim_b,)), ((), ())), preferred_element_type=jnp.float32)


def project_kernel(x_ref, w_ref, out_ref, stage):
    for pair in range(COLS // 2):
        rows = [x_ref[pl.ds(2 * pair + s, ROWS, stride=COLS), :] for s in range(2)]
        normed = norm_lanes(jnp.concatenate(rows, axis=0))
        swapped = normed.reshape(2, 4, 2, 16, CH).transpose(0, 2, 1, 3, 4).reshape(2 * ROWS, CH)
        for base, half, values in ((16, 0, normed), (0, 2 * CH, swapped)):
            p = contract(w_ref[half : half + 2 * CH, :], values, 1, 1)
            product = sigmoid(p[:CH]) * p[CH:]
            for s in range(2):
                stage[pl.ds(base + 2 * pair + s, CH, stride=2 * COLS), :] = product[:, s * ROWS : (s + 1) * ROWS]
    out_ref[...] = stage[...].astype(jnp.bfloat16).reshape(CH, 2 * COLS, ROWS)


def split_kernel(a_ref, own_ref, other_ref, core_ref):
    core = lax.axis_index("core")
    right = a_ref[:, :COLS, :].astype(jnp.float32).reshape(2, 2, 32 * COLS, ROWS)
    low, high = right[:, 0], right[:, 1]
    first = jnp.concatenate([low[..., :64], high[..., :64]], axis=-1)
    second = jnp.concatenate([low[..., 64:], high[..., 64:]], axis=-1)
    own = jnp.where(core == 0, first, second).astype(jnp.bfloat16).reshape(64, COLS, ROWS)
    other = jnp.where(core == 0, second, first).astype(jnp.bfloat16).reshape(64, COLS, ROWS)
    own_ref[...] = own
    other_ref[...] = other
    core_ref[:CH] = a_ref[:, COLS:, :]
    core_ref[CH:] = other


def triangle_kernel(a_ref, own_ref, core_ref, x_ref, xc_ref, out_ref):
    xb = lax.axis_index("xb")
    lefts = []
    for ref, base in ((a_ref, COLS), (core_ref, 0)):
        lefts.append(
            jnp.concatenate(
                [ref[32 * g : 32 * g + 32, base : base + COLS, :].reshape(32 * COLS, ROWS) for g in range(4)], axis=1
            )
        )
    for xh in range(2):
        total = None
        for left, parts in ((lefts[0], ((own_ref, 0), (x_ref, 0))), (lefts[1], ((core_ref, CH), (xc_ref, 0)))):
            right = jnp.concatenate(
                [ref[at + 32 * xh : at + 32 * xh + 32].reshape(32 * COLS, ROWS) for ref, at in parts], axis=1
            )
            term = contract(right, left, 0, 0)
            total = term if total is None else total + term
        total = total.astype(jnp.bfloat16)
        for rel in range(2):
            for zh in range(2):
                row = 128 * rel + 64 * zh
                y = 4 * xh + 2 * (xb if rel == 0 else 1 - xb) + zh
                for g in range(4):
                    out_ref[g, y] = total[row : row + 64, 128 * g : 128 * g + 128]


def finish_kernel(x_ref, t_ref, gate_ref, proj_ref, in_ref, down_ref, out_ref, stage):
    stage[...] = t_ref[...].astype(jnp.float32)
    hidden = down_ref.shape[0]
    for pair in range(COLS // 2):
        at = [2 * pair + s for s in range(2)]
        tri = jnp.concatenate([stage[pl.ds(j, CH, stride=COLS), :] for j in at], axis=1)
        centred = tri - jnp.mean(tri, axis=0, keepdims=True)
        spread = jnp.mean(centred * centred, axis=0, keepdims=True)
        tri_normed = (centred * lax.rsqrt(spread + EPS)).astype(jnp.bfloat16)
        x = jnp.concatenate([x_ref[pl.ds(j, ROWS, stride=COLS), :] for j in at], axis=0)
        gating = sigmoid(contract(norm_lanes(x), gate_ref[...], 1, 0))
        middle = x + gating * contract(tri_normed, proj_ref[...], 0, 0)
        t = contract(norm_lanes(middle), in_ref[...], 1, 0)
        up = t[:, :hidden]
        units = (up * sigmoid(up) * t[:, hidden:]).astype(jnp.bfloat16)
        result = middle + contract(units, down_ref[...], 1, 0)
        for s, j in enumerate(at):
            out_ref[pl.ds(j, ROWS, stride=COLS), :] = result[s * ROWS : (s + 1) * ROWS]


def call(kernel, outs, scratch=(), flops=0, moved=0):
    return pl.pallas_call(
        kernel,
        out_shape=outs,
        scratch_shapes=list(scratch),
        compiler_params=pltpu.CompilerParams(vmem_limit_bytes=LIMIT),
        cost_estimate=pl.CostEstimate(flops=flops, bytes_accessed=moved, transcendentals=0),
    )


def per_device(pair_rep, pair_proj, gate_proj, out_proj, trans_in, trans_out):
    bf16 = functools.partial(jax.ShapeDtypeStruct, dtype=jnp.bfloat16)
    flat = pair_rep.reshape(ROWS * COLS, CH)
    with jax.named_scope("project"):
        sides = call(
            project_kernel, bf16((CH, 2 * COLS, ROWS)), [pltpu.VMEM((CH * 2 * COLS, ROWS), jnp.float32)], 270_000_000, 2 << 20
        )(flat, pair_proj.T)
    with jax.named_scope("to_channels"):
        sides = lax.all_to_all(sides, PLANE, 0, 0, tiled=True)
    with jax.named_scope("split"):
        own, other, pack = call(
            split_kernel, (bf16((64, COLS, ROWS)), bf16((64, COLS, ROWS)), bf16((CH + 64, COLS, ROWS))), (), 0, 2 << 20
        )(sides)
    with jax.named_scope("share"):
        across = lax.ppermute(own, QUAD, [(d, d ^ 2) for d in range(4)])
        diagonal = lax.ppermute(other, QUAD, [(d, d ^ 3) for d in range(4)])
        pack = lax.ppermute(pack, QUAD, [(d, d ^ 1) for d in range(4)])
    with jax.named_scope("triangle"):
        tri = call(triangle_kernel, bf16((4, 8, 64, ROWS)), (), 540_000_000, 3 << 20)(sides, own, pack, across, diagonal)
    with jax.named_scope("to_columns"):
        tri = lax.all_to_all(tri.reshape(CH, COLS, ROWS), PLANE, 0, 0, tiled=True)
    with jax.named_scope("finish"):
        out = call(
            finish_kernel,
            jax.ShapeDtypeStruct((ROWS * COLS, CH), jnp.float32),
            [pltpu.VMEM((CH * COLS, ROWS), jnp.float32)],
            1_000_000_000,
            3 << 20,
        )(flat, tri.reshape(CH * COLS, ROWS), gate_proj, out_proj, trans_in, trans_out)
    return out.reshape(ROWS, COLS, CH)


def solution(mesh):
    fine = Mesh(mesh.devices.reshape(SIZES), AXES)
    spec = P(("xh", "xb", "zh"), ("y", "zl", "core"), None)
    return jax.shard_map(
        per_device, mesh=fine, in_specs=(spec, P(), P(), P(), P(), P()), out_specs=spec, check_vma=False
    )
```

```python
import functools

import jax
import jax.numpy as jnp
from jax import lax
from jax.experimental import pallas as pl
from jax.experimental.pallas import tpu as pltpu
from jax.sharding import Mesh
from jax.sharding import PartitionSpec as P

AXES = ("xh", "xb", "zh", "y", "zl", "core")
SIZES = (2, 2, 2, 8, 4, 2)
PLANE = ("xh", "zh", "y", "zl")
QUAD = ("xb", "core")
ROWS = 128
COLS = 16
CH = 128
PAIRS = COLS // 2
EPS = 1e-05
LIMIT = 16 * 1024 * 1024


def sigmoid(v):
    return 0.5 * jnp.tanh(0.5 * v) + 0.5


def norm_rows(v):
    centred = v - jnp.mean(v, axis=0, keepdims=True)
    spread = jnp.mean(centred * centred, axis=0, keepdims=True)
    return (centred * lax.rsqrt(spread + EPS)).astype(jnp.bfloat16)


def dot(a, b):
    return jnp.dot(a, b, preferred_element_type=jnp.float32)


def columns(ref, pair):
    return jnp.concatenate([ref[pl.ds(2 * pair + s, ROWS, stride=COLS), :].T for s in range(2)], axis=1)


def project_kernel(x_ref, w_ref, out_ref, stage):
    weights = w_ref[...].T
    for pair in range(PAIRS):
        p = dot(weights, norm_rows(columns(x_ref, pair)))
        for base, at in ((COLS, 0), (0, 2 * CH)):
            product = sigmoid(p[at : at + CH]) * p[at + CH : at + 2 * CH]
            for s in range(2):
                stage[pl.ds(base + 2 * pair + s, CH, stride=2 * COLS), :] = product[:, s * ROWS : (s + 1) * ROWS]
    out_ref[...] = stage[...].astype(jnp.bfloat16).reshape(CH, 2 * COLS, ROWS)


def gate_kernel(x_ref, gate_ref, proj_ref, in_ref, down_ref, xt_ref, gating_ref, proj_t_ref, in_t_ref, down_t_ref):
    weights = gate_ref[...].T
    for pair in range(PAIRS):
        xt = columns(x_ref, pair)
        xt_ref[pair] = xt
        gating_ref[pair] = sigmoid(dot(weights, norm_rows(xt)))
    proj_t_ref[...] = proj_ref[...].T
    in_t_ref[...] = in_ref[...].T
    down_t_ref[...] = down_ref[...].T


def triangle_kernel(left_ref, right_ref, keep_ref, send_ref):
    core = lax.axis_index("core")
    left = jnp.concatenate(
        [left_ref[32 * g : 32 * g + 32, COLS:, :].reshape(32 * COLS, ROWS) for g in range(4)], axis=1
    )
    for xh in range(2):
        right = jnp.concatenate(
            [right_ref[64 * xh + 32 * zh : 64 * xh + 32 * zh + 32].reshape(32 * COLS, ROWS) for zh in range(2)], axis=1
        )
        part = lax.dot_general(right, left, (((0,), (0,)), ((), ())), preferred_element_type=jnp.float32)
        part = part.astype(jnp.bfloat16).reshape(2, 4, 2, 16, 4 * ROWS)
        first, second = part[:, :, 0], part[:, :, 1]
        keep = jnp.where(core == 0, first, second)
        send = jnp.where(core == 0, second, first)
        for g in range(4):
            keep_ref[g, xh] = keep[..., g * ROWS : (g + 1) * ROWS]
            send_ref[g, xh] = send[..., g * ROWS : (g + 1) * ROWS]


def add_kernel(keep_ref, got_ref, keep_x_ref, got_x_ref, out_ref):
    xb = lax.axis_index("xb")
    for a, b, at in ((keep_ref, got_ref, xb), (keep_x_ref, got_x_ref, 1 - xb)):
        for xh in range(2):
            for zh in range(2):
                total = a[:, xh, zh].astype(jnp.float32) + b[:, xh, zh].astype(jnp.float32)
                out_ref[:, 4 * xh + 2 * at + zh] = total.astype(jnp.bfloat16)


def finish_kernel(xt_ref, gating_ref, t_ref, proj_ref, in_ref, down_ref, out_ref, stage):
    stage[...] = t_ref[...].astype(jnp.float32)
    hidden = down_ref.shape[1]
    for pair in range(PAIRS):
        at = [2 * pair + s for s in range(2)]
        tri = jnp.concatenate([stage[pl.ds(j, CH, stride=COLS), :] for j in at], axis=1)
        middle = xt_ref[pair] + gating_ref[pair] * dot(proj_ref[...], norm_rows(tri))
        t = dot(in_ref[...], norm_rows(middle))
        up = t[:hidden]
        units = (up * sigmoid(up) * t[hidden:]).astype(jnp.bfloat16)
        result = middle + dot(down_ref[...], units)
        for s, j in enumerate(at):
            out_ref[pl.ds(j, ROWS, stride=COLS), :] = result[:, s * ROWS : (s + 1) * ROWS].T


def call(kernel, outs, scratch=(), flops=0, moved=0):
    return pl.pallas_call(
        kernel,
        out_shape=outs,
        scratch_shapes=list(scratch),
        compiler_params=pltpu.CompilerParams(vmem_limit_bytes=LIMIT),
        cost_estimate=pl.CostEstimate(flops=flops, bytes_accessed=moved, transcendentals=0),
    )


def per_device(pair_rep, pair_proj, gate_proj, out_proj, trans_in, trans_out):
    bf16 = functools.partial(jax.ShapeDtypeStruct, dtype=jnp.bfloat16)
    f32 = functools.partial(jax.ShapeDtypeStruct, dtype=jnp.float32)
    flat = pair_rep.reshape(ROWS * COLS, CH)
    with jax.named_scope("project"):
        sides = call(
            project_kernel, bf16((CH, 2 * COLS, ROWS)), [pltpu.VMEM((CH * 2 * COLS, ROWS), jnp.float32)], 270_000_000, 2 << 20
        )(flat, pair_proj)
    flat, sides = lax.optimization_barrier((flat, sides))
    with jax.named_scope("gate"):
        wide = f32((PAIRS, CH, 2 * ROWS))
        xt, gating, proj_t, in_t, down_t = call(
            gate_kernel,
            (wide, wide, bf16(out_proj.shape[::-1]), bf16(trans_in.shape[::-1]), bf16(trans_out.shape[::-1])),
            (),
            70_000_000,
            4 << 20,
        )(flat, gate_proj, out_proj, trans_in, trans_out)
    with jax.named_scope("to_channels"):
        sides = lax.all_to_all(sides, PLANE, 0, 0, tiled=True)
    with jax.named_scope("right_values"):
        right = sides[:, :COLS]
    with jax.named_scope("right_across_x"):
        right_x = lax.ppermute(right, QUAD, [(d, d ^ 2) for d in range(4)])
    part = bf16((4, 2, 2, 4, 16, ROWS))
    with jax.named_scope("triangle_own"):
        keep, send = call(triangle_kernel, (part, part), (), 270_000_000, 2 << 20)(sides, right)
    with jax.named_scope("sums_to_core"):
        got = lax.ppermute(send, QUAD, [(d, d ^ 1) for d in range(4)])
    with jax.named_scope("triangle_across"):
        keep_x, send_x = call(triangle_kernel, (part, part), (), 270_000_000, 2 << 20)(sides, right_x)
    with jax.named_scope("sums_to_core_across"):
        got_x = lax.ppermute(send_x, QUAD, [(d, d ^ 1) for d in range(4)])
    with jax.named_scope("add"):
        tri = call(add_kernel, bf16((4, 8, 4, 16, ROWS)), (), 1_000_000, 2 << 20)(keep, got, keep_x, got_x)
    with jax.named_scope("to_columns"):
        tri = lax.all_to_all(tri.reshape(CH, COLS, ROWS), PLANE, 0, 0, tiled=True)
    with jax.named_scope("finish"):
        out = call(
            finish_kernel,
            f32((ROWS * COLS, CH)),
            [pltpu.VMEM((CH * COLS, ROWS), jnp.float32)],
            1_000_000_000,
            4 << 20,
        )(xt, gating, tri.reshape(CH * COLS, ROWS), proj_t, in_t, down_t)
    return out.reshape(ROWS, COLS, CH)


def solution(mesh):
    fine = Mesh(mesh.devices.reshape(SIZES), AXES)
    spec = P(("xh", "xb", "zh"), ("y", "zl", "core"), None)
    return jax.shard_map(
        per_device, mesh=fine, in_specs=(spec, P(), P(), P(), P(), P()), out_specs=spec, check_vma=False
    )
```

```python
import functools

import jax
import jax.numpy as jnp
from jax import lax
from jax.experimental import pallas as pl
from jax.experimental.pallas import tpu as pltpu
from jax.sharding import Mesh
from jax.sharding import PartitionSpec as P

AXES = ("xh", "xb", "zh", "y", "zl", "core")
SIZES = (2, 2, 2, 8, 4, 2)
PLANE = ("xh", "zh", "y", "zl")
QUAD = ("xb", "core")
ROWS = 128
COLS = 16
CH = 128
HALF = COLS // 2
SIDES = 2 * COLS + 8
SUMS = COLS + 8
EPS = 1e-05
LIMIT = 16 * 1024 * 1024


def sigmoid(v):
    return 0.5 * jnp.tanh(0.5 * v) + 0.5


def norm_rows(v):
    centred = v - jnp.mean(v, axis=0, keepdims=True)
    spread = jnp.mean(centred * centred, axis=0, keepdims=True)
    return (centred * lax.rsqrt(spread + EPS)).astype(jnp.bfloat16)


def dot(a, b):
    return jnp.dot(a, b, preferred_element_type=jnp.float32)


def half_columns(ref, h):
    return jnp.concatenate([ref[pl.ds(HALF * h + s, ROWS, stride=COLS), :].T for s in range(HALF)], axis=1)


def project_kernel(x_ref, w_ref, out_ref, stage):
    weights = w_ref[...].T
    for h in range(2):
        p = dot(weights, norm_rows(half_columns(x_ref, h)))
        for base, at in ((COLS, 0), (0, 2 * CH)):
            product = sigmoid(p[at : at + CH]) * p[at + CH : at + 2 * CH]
            for s in range(HALF):
                stage[pl.ds(base + HALF * h + s, CH, stride=SIDES), :] = product[:, s * ROWS : (s + 1) * ROWS]
    out_ref[...] = stage[...].reshape(CH, SIDES, ROWS)[:, : 2 * COLS].astype(jnp.bfloat16)


def gate_kernel(x_ref, gate_ref, proj_ref, in_ref, down_ref, xt_ref, gating_ref, proj_t_ref, in_t_ref, down_t_ref):
    weights = gate_ref[...].T
    for h in range(2):
        xt = half_columns(x_ref, h)
        xt_ref[h] = xt
        gating_ref[h] = sigmoid(dot(weights, norm_rows(xt)))
    proj_t_ref[...] = proj_ref[...].T
    in_t_ref[...] = in_ref[...].T
    down_t_ref[...] = down_ref[...].T


def triangle_kernel(left_ref, right_ref, keep_ref, send_ref):
    core = lax.axis_index("core")
    left = jnp.concatenate(
        [left_ref[32 * g : 32 * g + 32, COLS:, :].reshape(32 * COLS, ROWS) for g in range(4)], axis=1
    )
    for xh in range(2):
        right = jnp.concatenate(
            [right_ref[64 * xh + 32 * zh : 64 * xh + 32 * zh + 32].reshape(32 * COLS, ROWS) for zh in range(2)], axis=1
        )
        part = lax.dot_general(right, left, (((0,), (0,)), ((), ())), preferred_element_type=jnp.float32)
        part = part.astype(jnp.bfloat16).reshape(2, 4, 2, 16, 4 * ROWS)
        first, second = part[:, :, 0], part[:, :, 1]
        keep = jnp.where(core == 0, first, second)
        send = jnp.where(core == 0, second, first)
        for g in range(4):
            keep_ref[g, xh] = keep[..., g * ROWS : (g + 1) * ROWS]
            send_ref[g, xh] = send[..., g * ROWS : (g + 1) * ROWS]


def add_kernel(keep_ref, got_ref, keep_x_ref, got_x_ref, out_ref):
    xb = lax.axis_index("xb")
    for a, b, at in ((keep_ref, got_ref, xb), (keep_x_ref, got_x_ref, 1 - xb)):
        for xh in range(2):
            for zh in range(2):
                total = a[:, xh, zh].astype(jnp.float32) + b[:, xh, zh].astype(jnp.float32)
                out_ref[:, 4 * xh + 2 * at + zh] = total.astype(jnp.bfloat16)


def finish_kernel(xt_ref, gating_ref, t_ref, proj_ref, in_ref, down_ref, out_hbm, stage, held, sems):
    stage[:, :COLS] = t_ref[...].astype(jnp.float32)
    rows = stage.reshape(CH * SUMS, ROWS)
    hidden = down_ref.shape[1]
    copies = []
    for h in range(2):
        tri = jnp.concatenate([rows[pl.ds(HALF * h + s, CH, stride=SUMS), :] for s in range(HALF)], axis=1)
        middle = xt_ref[h] + gating_ref[h] * dot(proj_ref[...], norm_rows(tri))
        t = dot(in_ref[...], norm_rows(middle))
        up = t[:hidden]
        units = (up * sigmoid(up) * t[hidden:]).astype(jnp.bfloat16)
        result = middle + dot(down_ref[...], units)
        for s in range(HALF):
            held.at[h][pl.ds(s, ROWS, stride=HALF), :] = result[:, s * ROWS : (s + 1) * ROWS].T
        copy = pltpu.make_async_copy(
            held.at[h].reshape(ROWS, HALF, CH), out_hbm.at[:, pl.ds(HALF * h, HALF), :], sems.at[h]
        )
        copy.start()
        copies.append(copy)
    for copy in copies:
        copy.wait()


VMEM = pl.BlockSpec(memory_space=pltpu.VMEM)
HBM = pl.BlockSpec(memory_space=pltpu.HBM)
HELD = pltpu.VMEM((2, ROWS * HALF, CH), jnp.float32)


def call(kernel, ins, outs, scratch=(), flops=0, moved=0, out_specs=None):
    many = isinstance(outs, tuple)
    return pl.pallas_call(
        kernel,
        out_shape=outs,
        in_specs=ins,
        out_specs=out_specs if out_specs is not None else ((VMEM,) * len(outs) if many else VMEM),
        scratch_shapes=list(scratch),
        compiler_params=pltpu.CompilerParams(vmem_limit_bytes=LIMIT),
        cost_estimate=pl.CostEstimate(flops=flops, bytes_accessed=moved, transcendentals=0),
    )


def per_device(pair_rep, pair_proj, gate_proj, out_proj, trans_in, trans_out):
    bf16 = functools.partial(jax.ShapeDtypeStruct, dtype=jnp.bfloat16)
    f32 = functools.partial(jax.ShapeDtypeStruct, dtype=jnp.float32)
    flat = pair_rep.reshape(ROWS * COLS, CH)
    with jax.named_scope("project"):
        sides = call(
            project_kernel,
            [VMEM, VMEM],
            bf16((CH, 2 * COLS, ROWS)),
            [pltpu.VMEM((CH * SIDES, ROWS), jnp.float32)],
            270_000_000,
            2 << 20,
        )(flat, pair_proj)
    with jax.named_scope("to_channels"):
        sides = lax.all_to_all(sides, PLANE, 0, 0, tiled=True)
    with jax.named_scope("right_values"):
        right = sides[:, :COLS]
    with jax.named_scope("right_across_x"):
        right_x = lax.ppermute(right, QUAD, [(d, d ^ 2) for d in range(4)])
    part = bf16((4, 2, 2, 4, 16, ROWS))
    with jax.named_scope("triangle_own"):
        keep, send = call(triangle_kernel, [VMEM] * 2, (part, part), (), 270_000_000, 2 << 20)(sides, right)
    with jax.named_scope("sums_to_core"):
        got = lax.ppermute(send, QUAD, [(d, d ^ 1) for d in range(4)])
    flat, keep = lax.optimization_barrier((flat, keep))
    with jax.named_scope("gate"):
        wide = f32((2, CH, HALF * ROWS))
        gate = call(
            gate_kernel,
            [VMEM] * 5,
            (wide, wide, bf16(out_proj.shape[::-1]), bf16(trans_in.shape[::-1]), bf16(trans_out.shape[::-1])),
            (),
            70_000_000,
            4 << 20,
        )(flat, gate_proj, out_proj, trans_in, trans_out)
    right_x, gate = lax.optimization_barrier((right_x, gate))
    with jax.named_scope("triangle_across"):
        keep_x, send_x = call(triangle_kernel, [VMEM] * 2, (part, part), (), 270_000_000, 2 << 20)(sides, right_x)
    with jax.named_scope("sums_to_core_across"):
        got_x = lax.ppermute(send_x, QUAD, [(d, d ^ 1) for d in range(4)])
    with jax.named_scope("add"):
        tri = call(add_kernel, [VMEM] * 4, bf16((4, 8, 4, 16, ROWS)), (), 1_000_000, 2 << 20)(keep, got, keep_x, got_x)
    with jax.named_scope("to_columns"):
        tri = lax.all_to_all(tri.reshape(CH, COLS, ROWS), PLANE, 0, 0, tiled=True)
    with jax.named_scope("finish"):
        xt, gating, proj_t, in_t, down_t = gate
        return call(
            finish_kernel,
            [VMEM] * 6,
            f32((ROWS, COLS, CH)),
            [pltpu.VMEM((CH, SUMS, ROWS), jnp.float32), HELD, pltpu.SemaphoreType.DMA((2,))],
            1_000_000_000,
            4 << 20,
            HBM,
        )(xt, gating, tri, proj_t, in_t, down_t)


def solution(mesh):
    fine = Mesh(mesh.devices.reshape(SIZES), AXES)
    spec = P(("xh", "xb", "zh"), ("y", "zl", "core"), None)
    return jax.shard_map(
        per_device, mesh=fine, in_specs=(spec, P(), P(), P(), P(), P()), out_specs=spec, check_vma=False
    )
```

```python
import functools

import jax
import jax.numpy as jnp
from jax import lax
from jax.experimental import pallas as pl
from jax.experimental.pallas import tpu as pltpu
from jax.sharding import Mesh
from jax.sharding import PartitionSpec as P

AXES = ("xh", "xb", "zh", "y", "zl", "core")
SIZES = (2, 2, 2, 8, 4, 2)
PLANE = ("y", "zh", "zl", "xb")
GROUP = (8, 2, 4, 2)
SHARE = ("xh", "xb", "core")
ROWS = 128
COLS = 16
CH = 128
HALF = COLS // 2
SIDES = 2 * COLS + 8
SUMS = COLS + 8
EPS = 1e-05
LIMIT = 16 * 1024 * 1024


def sigmoid(v):
    return 0.5 * jnp.tanh(0.5 * v) + 0.5


def norm_rows(v):
    centred = v - jnp.mean(v, axis=0, keepdims=True)
    spread = jnp.mean(centred * centred, axis=0, keepdims=True)
    return (centred * lax.rsqrt(spread + EPS)).astype(jnp.bfloat16)


def dot(a, b):
    return jnp.dot(a, b, preferred_element_type=jnp.float32)


def half_columns(ref, h):
    return jnp.concatenate([ref[pl.ds(HALF * h + s, ROWS, stride=COLS), :].T for s in range(HALF)], axis=1)


def project_kernel(x_ref, w_ref, out_ref, stage):
    weights = w_ref[...].T
    for h in range(2):
        p = dot(weights, norm_rows(half_columns(x_ref, h)))
        for base, at in ((COLS, 0), (0, 2 * CH)):
            product = sigmoid(p[at : at + CH]) * p[at + CH : at + 2 * CH]
            for s in range(HALF):
                stage[pl.ds(base + HALF * h + s, CH, stride=SIDES), :] = product[:, s * ROWS : (s + 1) * ROWS]
    xh = lax.axis_index("xh")
    for b in range(2):
        rows = stage[64 * SIDES * b : 64 * SIDES * (b + 1)].reshape(64, SIDES, ROWS)[:, : 2 * COLS]
        out_ref[:, jnp.bitwise_xor(xh, b)] = rows.astype(jnp.bfloat16)


def gate_kernel(x_ref, gate_ref, proj_ref, in_ref, down_ref, xt_ref, gating_ref, proj_t_ref, in_t_ref, down_t_ref):
    weights = gate_ref[...].T
    for h in range(2):
        xt = half_columns(x_ref, h)
        xt_ref[h] = xt
        gating_ref[h] = sigmoid(dot(weights, norm_rows(xt)))
    proj_t_ref[...] = proj_ref[...].T
    in_t_ref[...] = in_ref[...].T
    down_t_ref[...] = down_ref[...].T


def triangle_kernel(left_ref, right_ref, keep_ref, send_ref):
    core = lax.axis_index("core")
    left = left_ref[...].reshape(*GROUP, 2 * COLS, ROWS)
    left = jnp.concatenate(
        [left[:, zh, :, x, COLS:].reshape(32 * COLS, ROWS) for zh in range(2) for x in range(2)], axis=1
    )
    right = right_ref[...].reshape(*GROUP, COLS, ROWS)
    for xj in range(2):
        rows = jnp.concatenate([right[:, zj, :, xj].reshape(32 * COLS, ROWS) for zj in range(2)], axis=1)
        part = lax.dot_general(rows, left, (((0,), (0,)), ((), ())), preferred_element_type=jnp.float32)
        part = part.astype(jnp.bfloat16).reshape(2, 4, 2, 16, 4 * ROWS)
        first, second = part[:, :, 0], part[:, :, 1]
        keep = jnp.where(core == 0, first, second)
        send = jnp.where(core == 0, second, first)
        for zh in range(2):
            for x in range(2):
                at = slice((2 * zh + x) * ROWS, (2 * zh + x + 1) * ROWS)
                keep_ref[2 * xj : 2 * xj + 2, zh, :, x] = keep[..., at]
                send_ref[2 * xj : 2 * xj + 2, zh, :, x] = send[..., at]


def add_kernel(keep_ref, got_ref, keep_x_ref, got_x_ref, out_ref):
    xh = lax.axis_index("xh")
    for a, b, at in ((keep_ref, got_ref, xh), (keep_x_ref, got_x_ref, 1 - xh)):
        out_ref[at] = (a[...].astype(jnp.float32) + b[...].astype(jnp.float32)).astype(jnp.bfloat16)


def finish_kernel(xt_ref, gating_ref, t_ref, proj_ref, in_ref, down_ref, out_hbm, stage, held, sems):
    xh = lax.axis_index("xh")
    for b in range(2):
        stage[64 * b : 64 * b + 64, :COLS] = t_ref[:, jnp.bitwise_xor(xh, b)].astype(jnp.float32)
    rows = stage.reshape(CH * SUMS, ROWS)
    hidden = down_ref.shape[1]
    copies = []
    for h in range(2):
        tri = jnp.concatenate([rows[pl.ds(HALF * h + s, CH, stride=SUMS), :] for s in range(HALF)], axis=1)
        middle = xt_ref[h] + gating_ref[h] * dot(proj_ref[...], norm_rows(tri))
        t = dot(in_ref[...], norm_rows(middle))
        up = t[:hidden]
        units = (up * sigmoid(up) * t[hidden:]).astype(jnp.bfloat16)
        result = middle + dot(down_ref[...], units)
        for s in range(HALF):
            held.at[h][pl.ds(s, ROWS, stride=HALF), :] = result[:, s * ROWS : (s + 1) * ROWS].T
        copy = pltpu.make_async_copy(
            held.at[h].reshape(ROWS, HALF, CH), out_hbm.at[:, pl.ds(HALF * h, HALF), :], sems.at[h]
        )
        copy.start()
        copies.append(copy)
    for copy in copies:
        copy.wait()


VMEM = pl.BlockSpec(memory_space=pltpu.VMEM)
HBM = pl.BlockSpec(memory_space=pltpu.HBM)
HELD = pltpu.VMEM((2, ROWS * HALF, CH), jnp.float32)


def call(kernel, ins, outs, scratch=(), flops=0, moved=0, out_specs=None):
    many = isinstance(outs, tuple)
    return pl.pallas_call(
        kernel,
        out_shape=outs,
        in_specs=ins,
        out_specs=out_specs if out_specs is not None else ((VMEM,) * len(outs) if many else VMEM),
        scratch_shapes=list(scratch),
        compiler_params=pltpu.CompilerParams(vmem_limit_bytes=LIMIT),
        cost_estimate=pl.CostEstimate(flops=flops, bytes_accessed=moved, transcendentals=0),
    )


def per_device(pair_rep, pair_proj, gate_proj, out_proj, trans_in, trans_out):
    bf16 = functools.partial(jax.ShapeDtypeStruct, dtype=jnp.bfloat16)
    f32 = functools.partial(jax.ShapeDtypeStruct, dtype=jnp.float32)
    flat = pair_rep.reshape(ROWS * COLS, CH)
    with jax.named_scope("project"):
        sides = call(
            project_kernel,
            [VMEM, VMEM],
            bf16((CH // 2, 2, 2 * COLS, ROWS)),
            [pltpu.VMEM((CH * SIDES, ROWS), jnp.float32)],
            270_000_000,
            2 << 20,
        )(flat, pair_proj)
    with jax.named_scope("to_channels"):
        sides = lax.all_to_all(sides.reshape(CH, 2 * COLS, ROWS), PLANE, 0, 0, tiled=True)
    with jax.named_scope("right_values"):
        right = sides[:, :COLS]
    with jax.named_scope("right_across_x"):
        right_x = lax.ppermute(right, SHARE, [(d, d ^ 6) for d in range(8)])
    part = bf16((4, 2, 4, 2, COLS, ROWS))
    with jax.named_scope("triangle_own"):
        keep, send = call(triangle_kernel, [VMEM] * 2, (part, part), (), 270_000_000, 2 << 20)(sides, right)
    with jax.named_scope("sums_to_core"):
        got = lax.ppermute(send, SHARE, [(d, d ^ 1) for d in range(8)])
    flat, keep = lax.optimization_barrier((flat, keep))
    with jax.named_scope("gate"):
        wide = f32((2, CH, HALF * ROWS))
        gate = call(
            gate_kernel,
            [VMEM] * 5,
            (wide, wide, bf16(out_proj.shape[::-1]), bf16(trans_in.shape[::-1]), bf16(trans_out.shape[::-1])),
            (),
            70_000_000,
            4 << 20,
        )(flat, gate_proj, out_proj, trans_in, trans_out)
    right_x, gate = lax.optimization_barrier((right_x, gate))
    with jax.named_scope("triangle_across"):
        keep_x, send_x = call(triangle_kernel, [VMEM] * 2, (part, part), (), 270_000_000, 2 << 20)(sides, right_x)
    with jax.named_scope("sums_to_core_across"):
        got_x = lax.ppermute(send_x, SHARE, [(d, d ^ 1) for d in range(8)])
    with jax.named_scope("add"):
        tri = call(add_kernel, [VMEM] * 4, bf16((2, 4, 2, 4, 2, COLS, ROWS)), (), 1_000_000, 2 << 20)(keep, got, keep_x, got_x)
    with jax.named_scope("to_columns"):
        tri = lax.all_to_all(tri.reshape(CH, COLS, ROWS), PLANE, 0, 0, tiled=True)
    with jax.named_scope("finish"):
        xt, gating, proj_t, in_t, down_t = gate
        return call(
            finish_kernel,
            [VMEM] * 6,
            f32((ROWS, COLS, CH)),
            [pltpu.VMEM((CH, SUMS, ROWS), jnp.float32), HELD, pltpu.SemaphoreType.DMA((2,))],
            1_000_000_000,
            4 << 20,
            HBM,
        )(xt, gating, tri.reshape(CH // 2, 2, COLS, ROWS), proj_t, in_t, down_t)


def solution(mesh):
    fine = Mesh(mesh.devices.reshape(SIZES), AXES)
    spec = P(("xh", "xb", "zh"), ("y", "zl", "core"), None)
    return jax.shard_map(
        per_device, mesh=fine, in_specs=(spec, P(), P(), P(), P(), P()), out_specs=spec, check_vma=False
    )
```

```python
import functools
import itertools

import jax
import jax.numpy as jnp
from jax import lax
from jax.experimental import pallas as pl
from jax.experimental.pallas import tpu as pltpu
from jax.sharding import Mesh
from jax.sharding import PartitionSpec as P

AXES = ("xh", "xb", "zh", "y2", "y1", "y0", "zl1", "zl0", "core")
PLANE = ("xb", "y0", "zl0", "y1", "zl1", "y2", "zh")
SHARE = ("xh", "xb", "core")
ROWS = 128
COLS = 16
CH = 128
HALF = COLS // 2
QUARTER = HALF // 2
SIDES = 2 * COLS + 8
SUMS = COLS + 8
EPS = 1e-05
LIMIT = 16 * 1024 * 1024


def sigmoid(v):
    return 0.5 * jnp.tanh(0.5 * v) + 0.5


def norm_rows(v):
    centred = v - jnp.mean(v, axis=0, keepdims=True)
    spread = jnp.mean(centred * centred, axis=0, keepdims=True)
    return (centred * lax.rsqrt(spread + EPS)).astype(jnp.bfloat16)


def dot(a, b):
    return jnp.dot(a, b, preferred_element_type=jnp.float32)


def half_columns(ref, h):
    return jnp.concatenate([ref[pl.ds(HALF * h + s, ROWS, stride=COLS), :].T for s in range(HALF)], axis=1)


def norm_kernel(x_ref, normed_ref):
    for h in range(2):
        normed_ref[h] = norm_rows(half_columns(x_ref, h))


def project_kernel(normed_ref, w_ref, out_ref, stage):
    weights = w_ref[...].T
    for h in range(2):
        p = dot(weights, normed_ref[h])
        for base, at in ((COLS, 0), (0, 2 * CH)):
            product = sigmoid(p[at : at + CH]) * p[at + CH : at + 2 * CH]
            for s in range(HALF):
                stage[pl.ds(base + HALF * h + s, CH, stride=SIDES), :] = product[:, s * ROWS : (s + 1) * ROWS]
    xh = lax.axis_index("xh")
    for b in range(2):
        rows = stage[64 * SIDES * b : 64 * SIDES * (b + 1)].reshape(64, SIDES, ROWS)[:, : 2 * COLS]
        out_ref[jnp.bitwise_xor(xh, b)] = rows.astype(jnp.bfloat16)


def gate_kernel(x_ref, gate_ref, proj_ref, in_ref, down_ref, xt_ref, gating_ref, proj_t_ref, in_t_ref, down_t_ref):
    weights = gate_ref[...].T
    for h in range(2):
        xt = half_columns(x_ref, h)
        xt_ref[h] = xt
        gating_ref[h] = sigmoid(dot(weights, norm_rows(xt)))
    proj_t_ref[...] = proj_ref[...].T
    in_t_ref[...] = in_ref[...].T
    down_t_ref[...] = down_ref[...].T


def triangle_kernel(left_ref, right_ref, keep_ref, send_ref):
    core = lax.axis_index("core")
    left = left_ref[...].reshape(2, 32, 2, 2 * COLS, ROWS)
    left = jnp.concatenate(
        [left[x, :, zh, COLS:].reshape(32 * COLS, ROWS) for zh in range(2) for x in range(2)], axis=1
    )
    right = right_ref[...].reshape(2, 32, 2, COLS, ROWS)
    for xj in range(2):
        rows = jnp.concatenate([right[xj, :, zj].reshape(32 * COLS, ROWS) for zj in range(2)], axis=1)
        part = lax.dot_general(rows, left, (((0,), (0,)), ((), ())), preferred_element_type=jnp.float32)
        part = part.astype(jnp.bfloat16).reshape(2, 4, 2, 16, 4 * ROWS)
        first, second = part[:, :, 0], part[:, :, 1]
        keep = jnp.where(core == 0, first, second)
        send = jnp.where(core == 0, second, first)
        for x, zj, z0, z1, zh in itertools.product(range(2), repeat=5):
            at = slice((2 * zh + x) * ROWS, (2 * zh + x + 1) * ROWS)
            to = 16 * x + 8 * zj + 4 * z0 + 2 * xj + z1
            keep_ref[to, zh] = keep[zj, 2 * z1 + z0, :, at]
            send_ref[to, zh] = send[zj, 2 * z1 + z0, :, at]


def add_kernel(keep_ref, got_ref, keep_x_ref, got_x_ref, out_ref):
    xh = lax.axis_index("xh")
    for a, b, at in ((keep_ref, got_ref, xh), (keep_x_ref, got_x_ref, 1 - xh)):
        out_ref[:, at] = (a[...].astype(jnp.float32) + b[...].astype(jnp.float32)).astype(jnp.bfloat16)


def finish_kernel(xt_ref, gating_ref, t_ref, proj_ref, in_ref, down_ref, out_hbm, stage, held, sems):
    xh = lax.axis_index("xh")
    for b in range(2):
        stage[64 * b : 64 * b + 64, :COLS] = t_ref[jnp.bitwise_xor(xh, b)].astype(jnp.float32)
    rows = stage.reshape(CH * SUMS, ROWS)
    hidden = down_ref.shape[1]
    copies = []
    for h in range(2):
        tri = jnp.concatenate([rows[pl.ds(HALF * h + s, CH, stride=SUMS), :] for s in range(HALF)], axis=1)
        middle = xt_ref[h] + gating_ref[h] * dot(proj_ref[...], norm_rows(tri))
        t = dot(in_ref[...], norm_rows(middle))
        up = t[:hidden]
        units = (up * sigmoid(up) * t[hidden:]).astype(jnp.bfloat16)
        result = middle + dot(down_ref[...], units)
        for q in range(2):
            for s in range(QUARTER):
                c = QUARTER * q + s
                held.at[h][pl.ds(c, ROWS, stride=HALF), :] = result[:, c * ROWS : (c + 1) * ROWS].T
            copy = pltpu.make_async_copy(
                held.at[h].reshape(ROWS, HALF, CH).at[:, pl.ds(QUARTER * q, QUARTER), :],
                out_hbm.at[:, pl.ds(HALF * h + QUARTER * q, QUARTER), :],
                sems.at[2 * h + q],
            )
            copy.start()
            copies.append(copy)
    for copy in copies:
        copy.wait()


VMEM = pl.BlockSpec(memory_space=pltpu.VMEM)
HBM = pl.BlockSpec(memory_space=pltpu.HBM)
HELD = pltpu.VMEM((2, ROWS * HALF, CH), jnp.float32)


def call(kernel, ins, outs, scratch=(), flops=0, moved=0, out_specs=None):
    many = isinstance(outs, tuple)
    return pl.pallas_call(
        kernel,
        out_shape=outs,
        in_specs=ins,
        out_specs=out_specs if out_specs is not None else ((VMEM,) * len(outs) if many else VMEM),
        scratch_shapes=list(scratch),
        compiler_params=pltpu.CompilerParams(vmem_limit_bytes=LIMIT),
        cost_estimate=pl.CostEstimate(flops=flops, bytes_accessed=moved, transcendentals=0),
    )


def per_device(pair_rep, pair_proj, gate_proj, out_proj, trans_in, trans_out):
    bf16 = functools.partial(jax.ShapeDtypeStruct, dtype=jnp.bfloat16)
    f32 = functools.partial(jax.ShapeDtypeStruct, dtype=jnp.float32)
    flat = pair_rep.reshape(ROWS * COLS, CH)
    with jax.named_scope("norm"):
        normed = call(norm_kernel, [VMEM], bf16((2, CH, HALF * ROWS)), (), 2_000_000, 2 << 20)(flat)
    with jax.named_scope("project"):
        sides = call(
            project_kernel,
            [VMEM, VMEM],
            bf16((2, CH // 2, 2 * COLS, ROWS)),
            [pltpu.VMEM((CH * SIDES, ROWS), jnp.float32)],
            270_000_000,
            2 << 20,
        )(normed, pair_proj)
    with jax.named_scope("to_channels"):
        sides = lax.all_to_all(sides.reshape(CH, 2 * COLS, ROWS), PLANE, 0, 0, tiled=True)
    with jax.named_scope("right_values"):
        right = sides[:, :COLS]
    with jax.named_scope("right_across_x"):
        right_x = lax.ppermute(right, SHARE, [(d, d ^ 6) for d in range(8)])
    part = bf16((32, 2, COLS, ROWS))
    with jax.named_scope("triangle_own"):
        keep, send = call(triangle_kernel, [VMEM] * 2, (part, part), (), 270_000_000, 2 << 20)(sides, right)
    with jax.named_scope("sums_to_core"):
        got = lax.ppermute(send, SHARE, [(d, d ^ 1) for d in range(8)])
    flat, keep = lax.optimization_barrier((flat, keep))
    with jax.named_scope("gate"):
        wide = f32((2, CH, HALF * ROWS))
        gate = call(
            gate_kernel,
            [VMEM] * 5,
            (wide, wide, bf16(out_proj.shape[::-1]), bf16(trans_in.shape[::-1]), bf16(trans_out.shape[::-1])),
            (),
            70_000_000,
            4 << 20,
        )(flat, gate_proj, out_proj, trans_in, trans_out)
    right_x, gate = lax.optimization_barrier((right_x, gate))
    with jax.named_scope("triangle_across"):
        keep_x, send_x = call(triangle_kernel, [VMEM] * 2, (part, part), (), 270_000_000, 2 << 20)(sides, right_x)
    with jax.named_scope("sums_to_core_across"):
        got_x = lax.ppermute(send_x, SHARE, [(d, d ^ 1) for d in range(8)])
    with jax.named_scope("add"):
        tri = call(add_kernel, [VMEM] * 4, bf16((32, 2, 2, COLS, ROWS)), (), 1_000_000, 2 << 20)(keep, got, keep_x, got_x)
    with jax.named_scope("to_columns"):
        tri = lax.all_to_all(tri.reshape(CH, COLS, ROWS), PLANE, 0, 0, tiled=True)
    with jax.named_scope("finish"):
        xt, gating, proj_t, in_t, down_t = gate
        return call(
            finish_kernel,
            [VMEM] * 6,
            f32((ROWS, COLS, CH)),
            [pltpu.VMEM((CH, SUMS, ROWS), jnp.float32), HELD, pltpu.SemaphoreType.DMA((4,))],
            1_000_000_000,
            4 << 20,
            HBM,
        )(xt, gating, tri.reshape(2, CH // 2, COLS, ROWS), proj_t, in_t, down_t)


def solution(mesh):
    fine = Mesh(mesh.devices.reshape((2,) * len(AXES)), AXES)
    spec = P(AXES[:3], AXES[3:], None)
    return jax.shard_map(
        per_device, mesh=fine, in_specs=(spec, P(), P(), P(), P(), P()), out_specs=spec, check_vma=False
    )
```

```python
import functools
import itertools

import jax
import jax.numpy as jnp
from jax import lax
from jax.experimental import pallas as pl
from jax.experimental.pallas import tpu as pltpu
from jax.sharding import Mesh
from jax.sharding import PartitionSpec as P

AXES = ("xh", "xb", "zh", "y2", "y1", "y0", "zl1", "zl0", "core")
PLANE = ("xb", "y0", "zl0", "y1", "zl1", "y2", "zh")
SHARE = ("xh", "xb", "core")
ROWS = 128
COLS = 16
CH = 128
HALF = COLS // 2
QUARTER = HALF // 2
SIDES = 2 * COLS + 8
SUMS = COLS + 8
EPS = 1e-05
FLOPS_X = 16_000_000_000
LIMIT = 16 * 1024 * 1024


def sigmoid(v):
    return 0.5 * jnp.tanh(0.5 * v) + 0.5


def norm_rows(v):
    centred = v - jnp.mean(v, axis=0, keepdims=True)
    spread = jnp.mean(centred * centred, axis=0, keepdims=True)
    return (centred * lax.rsqrt(spread + EPS)).astype(jnp.bfloat16)


def dot(a, b):
    return jnp.dot(a, b, preferred_element_type=jnp.float32)


def by_core(x):
    return x.reshape(4, 2, 16, CH).transpose(1, 0, 2, 3).reshape(2, 64, CH)


def half_columns(ref, h):
    return jnp.concatenate(
        [by_core(ref[pl.ds(HALF * h + s, ROWS, stride=COLS), :]).reshape(ROWS, CH).T for s in range(HALF)], axis=1
    )


def half_pairs(ref, h):
    tiles = []
    for pair in range(QUARTER):
        even, odd = (by_core(ref[pl.ds(HALF * h + 2 * pair + s, ROWS, stride=COLS), :]) for s in range(2))
        tiles += [jnp.concatenate([even[c], odd[c]], axis=0).T for c in range(2)]
    return jnp.concatenate(tiles, axis=1)


def norm_kernel(x_ref, normed_ref):
    for h in range(2):
        normed_ref[h] = norm_rows(half_pairs(x_ref, h))


def project_kernel(normed_ref, w_ref, out_ref, stage):
    core = lax.axis_index("core")
    weights = w_ref[...].T
    for h in range(2):
        p = dot(weights, normed_ref[h])
        left = sigmoid(p[:CH]) * p[CH : 2 * CH]
        right = sigmoid(p[2 * CH : 3 * CH]) * p[3 * CH :]
        for pair in range(QUARTER):
            row = QUARTER * h + pair
            for c in range(2):
                at = slice((2 * pair + c) * ROWS, (2 * pair + c + 1) * ROWS)
                stage[pl.ds(HALF * jnp.bitwise_xor(core, c) + row, CH, stride=SIDES), :] = right[:, at]
                stage[pl.ds(COLS + HALF * c + row, CH, stride=SIDES), :] = left[:, at]
    xh = lax.axis_index("xh")
    for b in range(2):
        rows = stage[64 * SIDES * b : 64 * SIDES * (b + 1)].reshape(64, SIDES, ROWS)[:, : 2 * COLS]
        out_ref[jnp.bitwise_xor(xh, b)] = rows.astype(jnp.bfloat16)


def gate_kernel(x_ref, gate_ref, proj_ref, in_ref, down_ref, xt_ref, gating_ref, proj_t_ref, in_t_ref, down_t_ref):
    weights = gate_ref[...].T
    for h in range(2):
        xt = half_columns(x_ref, h)
        xt_ref[h] = xt
        gating_ref[h] = sigmoid(dot(weights, norm_rows(xt)))
    proj_t_ref[...] = proj_ref[...].T
    in_t_ref[...] = in_ref[...].T
    down_t_ref[...] = down_ref[...].T


def halves(sides):
    low = lax.broadcasted_iota(jnp.int32, (32 * HALF, ROWS), 1) < 64
    parts = ([], [])
    for zh in range(2):
        for x in range(2):
            first = sides[x, :, zh, COLS : COLS + HALF].reshape(32 * HALF, ROWS)
            second = sides[x, :, zh, COLS + HALF :].reshape(32 * HALF, ROWS)
            parts[0].append(jnp.where(low, first, pltpu.roll(second, 64, 1)))
            parts[1].append(jnp.where(low, pltpu.roll(first, 64, 1), second))
    return [jnp.concatenate(part, axis=1).astype(jnp.bfloat16) for part in parts]


def turned(right):
    blocks = [right[x, :, zh].reshape(32 * HALF, ROWS).T for x in range(2) for zh in range(2)]
    return [
        jnp.concatenate([block[64 * s : 64 * s + 64] for block in blocks], axis=0).astype(jnp.bfloat16) for s in range(2)
    ]


def product(right, left):
    return dot(right[0], left[0]) + dot(right[1], left[1])


def wide(ref, rows):
    return ref[...].astype(jnp.float32).reshape(2, 32, 2, rows, ROWS)


def triangle_x_kernel(sides_ref, x_ref, left_ref, across_ref):
    left = halves(wide(sides_ref, 2 * COLS))
    for s in range(2):
        left_ref[s] = left[s]
    across_ref[...] = product(turned(wide(x_ref, HALF)), left)


def triangle_kernel(sides_ref, other_ref, xc_ref, left_ref, across_ref, out_ref):
    xh = lax.axis_index("xh")
    sides, other = wide(sides_ref, 2 * COLS), wide(other_ref, 2 * COLS)
    left, left_other = [left_ref[s] for s in range(2)], halves(other)
    own = product(turned(sides[:, :, :, :HALF]), left) + product(turned(other[:, :, :, HALF:COLS]), left_other)
    across = across_ref[...] + product(turned(wide(xc_ref, HALF)), left_other)
    for total, at in ((own, xh), (across, 1 - xh)):
        total = total.astype(jnp.bfloat16).reshape(2, 2, 4, 16, 4 * ROWS)
        for x, zj, z0, xj, z1, zh in itertools.product(range(2), repeat=6):
            lanes = slice((2 * zh + x) * ROWS, (2 * zh + x + 1) * ROWS)
            out_ref[16 * x + 8 * zj + 4 * z0 + 2 * xj + z1, at, zh] = total[xj, zj, 2 * z1 + z0, :, lanes]


def finish_kernel(xt_ref, gating_ref, t_ref, proj_ref, in_ref, down_ref, out_hbm, stage, held, sems):
    xh = lax.axis_index("xh")
    for b in range(2):
        stage[64 * b : 64 * b + 64, :COLS] = t_ref[jnp.bitwise_xor(xh, b)].astype(jnp.float32)
    sums = stage.reshape(CH * SUMS, ROWS)
    hidden = down_ref.shape[1]
    copies = []
    for h in range(2):
        tri = jnp.concatenate([sums[pl.ds(HALF * h + s, CH, stride=SUMS), :] for s in range(HALF)], axis=1)
        middle = xt_ref[h] + gating_ref[h] * dot(proj_ref[...], norm_rows(tri))
        t = dot(in_ref[...], norm_rows(middle))
        up = t[:hidden]
        units = (up * sigmoid(up) * t[hidden:]).astype(jnp.bfloat16)
        result = middle + dot(down_ref[...], units)
        for q in range(2):
            for s in range(QUARTER):
                c = QUARTER * q + s
                rows = result[:, c * ROWS : (c + 1) * ROWS].T.reshape(2, 4, 16, CH).transpose(1, 0, 2, 3)
                held.at[h][pl.ds(c, ROWS, stride=HALF), :] = rows.reshape(ROWS, CH)
            copy = pltpu.make_async_copy(
                held.at[h].reshape(ROWS, HALF, CH).at[:, pl.ds(QUARTER * q, QUARTER), :],
                out_hbm.at[:, pl.ds(HALF * h + QUARTER * q, QUARTER), :],
                sems.at[2 * h + q],
            )
            copy.start()
            copies.append(copy)
    for copy in copies:
        copy.wait()


VMEM = pl.BlockSpec(memory_space=pltpu.VMEM)
HBM = pl.BlockSpec(memory_space=pltpu.HBM)
HELD = pltpu.VMEM((2, ROWS * HALF, CH), jnp.float32)


def call(kernel, ins, outs, scratch=(), flops=0, moved=0, out_specs=None):
    many = isinstance(outs, tuple)
    return pl.pallas_call(
        kernel,
        out_shape=outs,
        in_specs=ins,
        out_specs=out_specs if out_specs is not None else ((VMEM,) * len(outs) if many else VMEM),
        scratch_shapes=list(scratch),
        compiler_params=pltpu.CompilerParams(vmem_limit_bytes=LIMIT),
        cost_estimate=pl.CostEstimate(flops=flops, bytes_accessed=moved, transcendentals=0),
    )


def per_device(pair_rep, pair_proj, gate_proj, out_proj, trans_in, trans_out):
    bf16 = functools.partial(jax.ShapeDtypeStruct, dtype=jnp.bfloat16)
    f32 = functools.partial(jax.ShapeDtypeStruct, dtype=jnp.float32)
    flat = pair_rep.reshape(ROWS * COLS, CH)
    with jax.named_scope("norm"):
        normed = call(norm_kernel, [VMEM], bf16((2, CH, HALF * ROWS)), (), 2_000_000, 2 << 20)(flat)
    with jax.named_scope("project"):
        sides = call(
            project_kernel,
            [VMEM, VMEM],
            bf16((2, CH // 2, 2 * COLS, ROWS)),
            [pltpu.VMEM((CH * SIDES, ROWS), jnp.float32)],
            270_000_000,
            2 << 20,
        )(normed, pair_proj)
    with jax.named_scope("to_channels"):
        sides = lax.all_to_all(sides.reshape(CH, 2 * COLS, ROWS), PLANE, 0, 0, tiled=True)
    flat, sides = lax.optimization_barrier((flat, sides))
    with jax.named_scope("right_across_x"):
        right_x = lax.ppermute(sides[:, :HALF].reshape(64, COLS, ROWS), SHARE, [(d, d ^ 6) for d in range(8)])
    with jax.named_scope("right_across_x_and_core"):
        right_xc = lax.ppermute(sides[:, HALF:COLS].reshape(64, COLS, ROWS), SHARE, [(d, d ^ 7) for d in range(8)])
    with jax.named_scope("sides_of_other_core"):
        other = lax.ppermute(sides, SHARE, [(d, d ^ 1) for d in range(8)])
    with jax.named_scope("gate"):
        turn = f32((2, CH, HALF * ROWS))
        gate = call(
            gate_kernel,
            [VMEM] * 5,
            (turn, turn, bf16(out_proj.shape[::-1]), bf16(trans_in.shape[::-1]), bf16(trans_out.shape[::-1])),
            (),
            70_000_000,
            4 << 20,
        )(flat, gate_proj, out_proj, trans_in, trans_out)
    right_x, right_xc, gate = lax.optimization_barrier((right_x, right_xc, gate))
    with jax.named_scope("triangle_x"):
        left, across = call(
            triangle_x_kernel, [VMEM] * 2, (bf16((2, 32 * HALF, 4 * ROWS)), f32((256, 4 * ROWS))), (), FLOPS_X, 3 << 20
        )(sides, right_x)
    left, across, other = lax.optimization_barrier((left, across, other))
    with jax.named_scope("triangle"):
        tri = call(triangle_kernel, [VMEM] * 5, bf16((32, 2, 2, COLS, ROWS)), (), 400_000_000, 4 << 20)(
            sides, other, right_xc, left, across
        )
    with jax.named_scope("to_columns"):
        tri = lax.all_to_all(tri.reshape(CH, COLS, ROWS), PLANE, 0, 0, tiled=True)
    with jax.named_scope("finish"):
        xt, gating, proj_t, in_t, down_t = gate
        return call(
            finish_kernel,
            [VMEM] * 6,
            f32((ROWS, COLS, CH)),
            [pltpu.VMEM((CH, SUMS, ROWS), jnp.float32), HELD, pltpu.SemaphoreType.DMA((4,))],
            1_000_000_000,
            4 << 20,
            HBM,
        )(xt, gating, tri.reshape(2, CH // 2, COLS, ROWS), proj_t, in_t, down_t)


def solution(mesh):
    fine = Mesh(mesh.devices.reshape((2,) * len(AXES)), AXES)
    spec = P(AXES[:3], AXES[3:], None)
    return jax.shard_map(
        per_device, mesh=fine, in_specs=(spec, P(), P(), P(), P(), P()), out_specs=spec, check_vma=False
    )
```

```python
import functools
import itertools

import jax
import jax.numpy as jnp
from jax import lax
from jax.experimental import pallas as pl
from jax.experimental.pallas import tpu as pltpu
from jax.sharding import Mesh
from jax.sharding import PartitionSpec as P

AXES = ("xh", "xb", "zh", "y2", "y1", "y0", "zl1", "zl0", "core")
PLANE = ("xb", "y0", "zl0", "y1", "zl1", "y2", "zh")
SHARE = ("xh", "xb", "core")
ROWS = 128
COLS = 16
CH = 128
HALF = COLS // 2
QUARTER = HALF // 2
SIDES = 2 * COLS + 8
SUMS = COLS + 8
EPS = 1e-05
FLOPS_X = 16_000_000_000
LIMIT = 16 * 1024 * 1024


def sigmoid(v):
    return 0.5 * jnp.tanh(0.5 * v) + 0.5


def norm_rows(v):
    centred = v - jnp.mean(v, axis=0, keepdims=True)
    spread = jnp.mean(centred * centred, axis=0, keepdims=True)
    return (centred * lax.rsqrt(spread + EPS)).astype(jnp.bfloat16)


def dot(a, b):
    return jnp.dot(a, b, preferred_element_type=jnp.float32)


def by_core(x):
    return x.reshape(4, 2, 16, CH).transpose(1, 0, 2, 3).reshape(2, 64, CH)


def half_columns(ref, h):
    return jnp.concatenate(
        [by_core(ref[pl.ds(HALF * h + s, ROWS, stride=COLS), :]).reshape(ROWS, CH).T for s in range(HALF)], axis=1
    )


def half_pairs(ref, h):
    tiles = []
    for pair in range(QUARTER):
        even, odd = (by_core(ref[pl.ds(HALF * h + 2 * pair + s, ROWS, stride=COLS), :]) for s in range(2))
        tiles += [jnp.concatenate([even[c], odd[c]], axis=0).T for c in range(2)]
    return jnp.concatenate(tiles, axis=1)


def norm_kernel(x_ref, normed_ref):
    for h in range(2):
        normed_ref[h] = norm_rows(half_pairs(x_ref, h))


def project_kernel(normed_ref, w_ref, out_ref, stage):
    core = lax.axis_index("core")
    weights = w_ref[...].T
    for h in range(2):
        p = dot(weights, normed_ref[h])
        left = sigmoid(p[:CH]) * p[CH : 2 * CH]
        right = sigmoid(p[2 * CH : 3 * CH]) * p[3 * CH :]
        for pair in range(QUARTER):
            row = QUARTER * h + pair
            for c in range(2):
                at = slice((2 * pair + c) * ROWS, (2 * pair + c + 1) * ROWS)
                stage[pl.ds(HALF * c + row, CH, stride=SIDES), :] = right[:, at]
                stage[pl.ds(COLS + HALF * c + row, CH, stride=SIDES), :] = left[:, at]
    xh = lax.axis_index("xh")
    for b in range(2):
        rows = stage[64 * SIDES * b : 64 * SIDES * (b + 1)].reshape(64, SIDES, ROWS)
        first, second = rows[:, :HALF], rows[:, HALF:COLS]
        own = jnp.where(core == 0, first, second)
        other = jnp.where(core == 0, second, first)
        rows = jnp.concatenate([own, other, rows[:, COLS : 2 * COLS]], axis=1)
        out_ref[jnp.bitwise_xor(xh, b)] = rows.astype(jnp.bfloat16)


def gate_kernel(x_ref, gate_ref, proj_ref, in_ref, down_ref, xt_ref, gating_ref, proj_t_ref, in_t_ref, down_t_ref):
    weights = gate_ref[...].T
    for h in range(2):
        xt = half_columns(x_ref, h)
        xt_ref[h] = xt
        gating_ref[h] = sigmoid(dot(weights, norm_rows(xt)))
    proj_t_ref[...] = proj_ref[...].T
    in_t_ref[...] = in_ref[...].T
    down_t_ref[...] = down_ref[...].T


def halves(sides):
    low = lax.broadcasted_iota(jnp.int32, (32 * HALF, ROWS), 1) < 64
    parts = ([], [])
    for zh in range(2):
        for x in range(2):
            first = sides[x, :, zh, COLS : COLS + HALF].reshape(32 * HALF, ROWS)
            second = sides[x, :, zh, COLS + HALF :].reshape(32 * HALF, ROWS)
            parts[0].append(jnp.where(low, first, pltpu.roll(second, 64, 1)))
            parts[1].append(jnp.where(low, pltpu.roll(first, 64, 1), second))
    return [jnp.concatenate(part, axis=1).astype(jnp.bfloat16) for part in parts]


def turned(right):
    blocks = [right[x, :, zh].reshape(32 * HALF, ROWS).T for x in range(2) for zh in range(2)]
    return [
        jnp.concatenate([block[64 * s : 64 * s + 64] for block in blocks], axis=0).astype(jnp.bfloat16) for s in range(2)
    ]


def product(right, left):
    return dot(right[0], left[0]) + dot(right[1], left[1])


def wide(ref, rows):
    return ref[...].astype(jnp.float32).reshape(2, 32, 2, rows, ROWS)


def triangle_own_kernel(sides_ref, left_ref, own_ref):
    sides = wide(sides_ref, 2 * COLS)
    left = halves(sides)
    for s in range(2):
        left_ref[s] = left[s]
    own_ref[...] = product(turned(sides[:, :, :, :HALF]), left)


def triangle_x_kernel(x_ref, left_ref, across_ref):
    across_ref[...] = product(turned(wide(x_ref, HALF)), [left_ref[s] for s in range(2)])


def triangle_kernel(other_ref, xc_ref, own_ref, across_ref, out_ref):
    xh = lax.axis_index("xh")
    other = wide(other_ref, 2 * COLS)
    left = halves(other)
    own = own_ref[...] + product(turned(other[:, :, :, HALF:COLS]), left)
    across = across_ref[...] + product(turned(wide(xc_ref, HALF)), left)
    for total, at in ((own, xh), (across, 1 - xh)):
        total = total.astype(jnp.bfloat16).reshape(2, 2, 4, 16, 4 * ROWS)
        for x, zj, z0, xj, z1, zh in itertools.product(range(2), repeat=6):
            lanes = slice((2 * zh + x) * ROWS, (2 * zh + x + 1) * ROWS)
            out_ref[16 * x + 8 * zj + 4 * z0 + 2 * xj + z1, at, zh] = total[xj, zj, 2 * z1 + z0, :, lanes]


def finish_kernel(xt_ref, gating_ref, t_ref, proj_ref, in_ref, down_ref, out_hbm, stage, held, sems):
    xh = lax.axis_index("xh")
    for b in range(2):
        stage[64 * b : 64 * b + 64, :COLS] = t_ref[jnp.bitwise_xor(xh, b)].astype(jnp.float32)
    sums = stage.reshape(CH * SUMS, ROWS)
    hidden = down_ref.shape[1]
    copies = []
    for h in range(2):
        tri = jnp.concatenate([sums[pl.ds(HALF * h + s, CH, stride=SUMS), :] for s in range(HALF)], axis=1)
        middle = xt_ref[h] + gating_ref[h] * dot(proj_ref[...], norm_rows(tri))
        t = dot(in_ref[...], norm_rows(middle))
        up = t[:hidden]
        units = (up * sigmoid(up) * t[hidden:]).astype(jnp.bfloat16)
        result = middle + dot(down_ref[...], units)
        for q in range(2):
            for s in range(QUARTER):
                c = QUARTER * q + s
                rows = result[:, c * ROWS : (c + 1) * ROWS].T.reshape(2, 4, 16, CH).transpose(1, 0, 2, 3)
                held.at[h][pl.ds(c, ROWS, stride=HALF), :] = rows.reshape(ROWS, CH)
            copy = pltpu.make_async_copy(
                held.at[h].reshape(ROWS, HALF, CH).at[:, pl.ds(QUARTER * q, QUARTER), :],
                out_hbm.at[:, pl.ds(HALF * h + QUARTER * q, QUARTER), :],
                sems.at[2 * h + q],
            )
            copy.start()
            copies.append(copy)
    for copy in copies:
        copy.wait()


VMEM = pl.BlockSpec(memory_space=pltpu.VMEM)
HBM = pl.BlockSpec(memory_space=pltpu.HBM)
HELD = pltpu.VMEM((2, ROWS * HALF, CH), jnp.float32)


def call(kernel, ins, outs, scratch=(), flops=0, moved=0, out_specs=None):
    many = isinstance(outs, tuple)
    return pl.pallas_call(
        kernel,
        out_shape=outs,
        in_specs=ins,
        out_specs=out_specs if out_specs is not None else ((VMEM,) * len(outs) if many else VMEM),
        scratch_shapes=list(scratch),
        compiler_params=pltpu.CompilerParams(vmem_limit_bytes=LIMIT),
        cost_estimate=pl.CostEstimate(flops=flops, bytes_accessed=moved, transcendentals=0),
    )


def per_device(pair_rep, pair_proj, gate_proj, out_proj, trans_in, trans_out):
    bf16 = functools.partial(jax.ShapeDtypeStruct, dtype=jnp.bfloat16)
    f32 = functools.partial(jax.ShapeDtypeStruct, dtype=jnp.float32)
    flat = pair_rep.reshape(ROWS * COLS, CH)
    with jax.named_scope("norm"):
        normed = call(norm_kernel, [VMEM], bf16((2, CH, HALF * ROWS)), (), 2_000_000, 2 << 20)(flat)
    with jax.named_scope("project"):
        sides = call(
            project_kernel,
            [VMEM, VMEM],
            bf16((2, CH // 2, 2 * COLS, ROWS)),
            [pltpu.VMEM((CH * SIDES, ROWS), jnp.float32)],
            270_000_000,
            2 << 20,
        )(normed, pair_proj)
    with jax.named_scope("to_channels"):
        sides = lax.all_to_all(sides.reshape(CH, 2 * COLS, ROWS), PLANE, 0, 0, tiled=True)
    flat, sides = lax.optimization_barrier((flat, sides))
    with jax.named_scope("right_across_x"):
        right_x = lax.ppermute(sides[:, :HALF].reshape(64, COLS, ROWS), SHARE, [(d, d ^ 6) for d in range(8)])
    with jax.named_scope("right_across_x_and_core"):
        right_xc = lax.ppermute(sides[:, HALF:COLS].reshape(64, COLS, ROWS), SHARE, [(d, d ^ 7) for d in range(8)])
    with jax.named_scope("sides_of_other_core"):
        other = lax.ppermute(sides, SHARE, [(d, d ^ 1) for d in range(8)])
    with jax.named_scope("gate"):
        turn = f32((2, CH, HALF * ROWS))
        gate = call(
            gate_kernel,
            [VMEM] * 5,
            (turn, turn, bf16(out_proj.shape[::-1]), bf16(trans_in.shape[::-1]), bf16(trans_out.shape[::-1])),
            (),
            70_000_000,
            4 << 20,
        )(flat, gate_proj, out_proj, trans_in, trans_out)
    with jax.named_scope("triangle_own"):
        sums = f32((256, 4 * ROWS))
        left, own = call(
            triangle_own_kernel, [VMEM], (bf16((2, 32 * HALF, 4 * ROWS)), sums), (), 140_000_000, 3 << 20
        )(sides)
    right_x, right_xc, left, own, gate = lax.optimization_barrier((right_x, right_xc, left, own, gate))
    with jax.named_scope("triangle_x"):
        across = call(triangle_x_kernel, [VMEM] * 2, sums, (), FLOPS_X, 2 << 20)(right_x, left)
    across, other = lax.optimization_barrier((across, other))
    with jax.named_scope("triangle"):
        tri = call(triangle_kernel, [VMEM] * 4, bf16((32, 2, 2, COLS, ROWS)), (), 280_000_000, 4 << 20)(
            other, right_xc, own, across
        )
    with jax.named_scope("to_columns"):
        tri = lax.all_to_all(tri.reshape(CH, COLS, ROWS), PLANE, 0, 0, tiled=True)
    with jax.named_scope("finish"):
        xt, gating, proj_t, in_t, down_t = gate
        return call(
            finish_kernel,
            [VMEM] * 6,
            f32((ROWS, COLS, CH)),
            [pltpu.VMEM((CH, SUMS, ROWS), jnp.float32), HELD, pltpu.SemaphoreType.DMA((4,))],
            1_000_000_000,
            4 << 20,
            HBM,
        )(xt, gating, tri.reshape(2, CH // 2, COLS, ROWS), proj_t, in_t, down_t)


def solution(mesh):
    fine = Mesh(mesh.devices.reshape((2,) * len(AXES)), AXES)
    spec = P(AXES[:3], AXES[3:], None)
    return jax.shard_map(
        per_device, mesh=fine, in_specs=(spec, P(), P(), P(), P(), P()), out_specs=spec, check_vma=False
    )
```

```python
import functools
import itertools

import jax
import jax.numpy as jnp
from jax import lax
from jax.experimental import pallas as pl
from jax.experimental.pallas import tpu as pltpu
from jax.sharding import Mesh
from jax.sharding import PartitionSpec as P

AXES = ("xh", "xb", "zh", "y2", "y1", "y0", "zl1", "zl0", "core")
PLANE = ("xb", "y0", "zl0", "y1", "zl1", "y2", "zh")
SHARE = ("xh", "xb", "core")
ROWS = 128
COLS = 16
CH = 128
HALF = COLS // 2
QUARTER = HALF // 2
SIDES = 2 * COLS + 8
SUMS = COLS + 8
EPS = 1e-05
FLOPS_X = 16_000_000_000
LIMIT = 16 * 1024 * 1024


def sigmoid(v):
    return 0.5 * jnp.tanh(0.5 * v) + 0.5


def norm_rows(v):
    centred = v - jnp.mean(v, axis=0, keepdims=True)
    spread = jnp.mean(centred * centred, axis=0, keepdims=True)
    return (centred * lax.rsqrt(spread + EPS)).astype(jnp.bfloat16)


def dot(a, b):
    return jnp.dot(a, b, preferred_element_type=jnp.float32)


def by_core(x):
    return x.reshape(4, 2, 16, CH).transpose(1, 0, 2, 3).reshape(2, 64, CH)


def half_columns(ref, h):
    return jnp.concatenate(
        [by_core(ref[pl.ds(HALF * h + s, ROWS, stride=COLS), :]).reshape(ROWS, CH).T for s in range(HALF)], axis=1
    )


def half_pairs(ref, h):
    tiles = []
    for pair in range(QUARTER):
        even, odd = (by_core(ref[pl.ds(HALF * h + 2 * pair + s, ROWS, stride=COLS), :]) for s in range(2))
        tiles += [jnp.concatenate([even[c], odd[c]], axis=0).T for c in range(2)]
    return jnp.concatenate(tiles, axis=1)


def norm_kernel(x_ref, normed_ref):
    for h in range(2):
        normed_ref[h] = norm_rows(half_pairs(x_ref, h))


def project_kernel(normed_ref, w_ref, out_ref, stage):
    core = lax.axis_index("core")
    weights = w_ref[...].T
    for h in range(2):
        p = dot(weights, normed_ref[h])
        left = sigmoid(p[:CH]) * p[CH : 2 * CH]
        right = sigmoid(p[2 * CH : 3 * CH]) * p[3 * CH :]
        for pair in range(QUARTER):
            row = QUARTER * h + pair
            for c in range(2):
                at = slice((2 * pair + c) * ROWS, (2 * pair + c + 1) * ROWS)
                stage[pl.ds(HALF * c + row, CH, stride=SIDES), :] = right[:, at]
                stage[pl.ds(COLS + HALF * c + row, CH, stride=SIDES), :] = left[:, at]
    xh = lax.axis_index("xh")
    for b in range(2):
        rows = stage[64 * SIDES * b : 64 * SIDES * (b + 1)].reshape(64, SIDES, ROWS)
        first, second = rows[:, :HALF], rows[:, HALF:COLS]
        own = jnp.where(core == 0, first, second)
        other = jnp.where(core == 0, second, first)
        rows = jnp.concatenate([own, other, rows[:, COLS : 2 * COLS]], axis=1)
        out_ref[jnp.bitwise_xor(xh, b)] = rows.astype(jnp.bfloat16)


def gate_kernel(x_ref, gate_ref, proj_ref, in_ref, down_ref, xt_ref, gating_ref, proj_t_ref, in_t_ref, down_t_ref):
    weights = gate_ref[...].T
    for h in range(2):
        xt = half_columns(x_ref, h)
        xt_ref[h] = xt
        gating_ref[h] = sigmoid(dot(weights, norm_rows(xt)))
    proj_t_ref[...] = proj_ref[...].T
    in_t_ref[...] = in_ref[...].T
    down_t_ref[...] = down_ref[...].T


def halves(sides):
    low = lax.broadcasted_iota(jnp.int32, (32 * HALF, ROWS), 1) < 64
    parts = ([], [])
    for zh in range(2):
        for x in range(2):
            first = sides[x, :, zh, COLS : COLS + HALF].reshape(32 * HALF, ROWS)
            second = sides[x, :, zh, COLS + HALF :].reshape(32 * HALF, ROWS)
            parts[0].append(jnp.where(low, first, pltpu.roll(second, 64, 1)))
            parts[1].append(jnp.where(low, pltpu.roll(first, 64, 1), second))
    return [jnp.concatenate(part, axis=1).astype(jnp.bfloat16) for part in parts]


def turned(right):
    blocks = [right[x, :, zh].reshape(32 * HALF, ROWS).astype(jnp.bfloat16).T for x in range(2) for zh in range(2)]
    return [
        jnp.concatenate([block[64 * s : 64 * s + 64] for block in blocks], axis=0) for s in range(2)
    ]


def product(right, left):
    return dot(right[0], left[0]) + dot(right[1], left[1])


def wide(ref, rows):
    return ref[...].astype(jnp.float32).reshape(2, 32, 2, rows, ROWS)


LEFT = 4 * ROWS


def triangle_own_kernel(sides_ref, pack_ref, own_ref):
    sides = wide(sides_ref, 2 * COLS)
    left, right = halves(sides), turned(sides[:, :, :, HALF:COLS])
    for s in range(2):
        pack_ref[s, :, :LEFT] = left[s]
        pack_ref[s, :, LEFT:] = right[s]
    own_ref[...] = product(turned(sides[:, :, :, :HALF]), left)


def triangle_x_kernel(x_ref, pack_ref, across_ref):
    across_ref[...] = product(turned(wide(x_ref, HALF)), [pack_ref[s, :, :LEFT] for s in range(2)])


def triangle_kernel(other_ref, xc_ref, own_ref, across_ref, out_ref):
    xh = lax.axis_index("xh")
    left = [other_ref[s, :, :LEFT] for s in range(2)]
    own = own_ref[...] + product([other_ref[s, :, LEFT:] for s in range(2)], left)
    across = across_ref[...] + product(turned(wide(xc_ref, HALF)), left)
    for total, at in ((own, xh), (across, 1 - xh)):
        total = total.astype(jnp.bfloat16).reshape(2, 2, 4, 16, 4 * ROWS)
        for x, zj, z0, xj, z1, zh in itertools.product(range(2), repeat=6):
            lanes = slice((2 * zh + x) * ROWS, (2 * zh + x + 1) * ROWS)
            out_ref[16 * x + 8 * zj + 4 * z0 + 2 * xj + z1, at, zh] = total[xj, zj, 2 * z1 + z0, :, lanes]


def finish_kernel(xt_ref, gating_ref, t_ref, proj_ref, in_ref, down_ref, out_hbm, stage, held, sems):
    xh = lax.axis_index("xh")
    for b in range(2):
        stage[64 * b : 64 * b + 64, :COLS] = t_ref[jnp.bitwise_xor(xh, b)].astype(jnp.float32)
    sums = stage.reshape(CH * SUMS, ROWS)
    hidden = down_ref.shape[1]
    copies = []
    for h in range(2):
        tri = jnp.concatenate([sums[pl.ds(HALF * h + s, CH, stride=SUMS), :] for s in range(HALF)], axis=1)
        middle = xt_ref[h] + gating_ref[h] * dot(proj_ref[...], norm_rows(tri))
        t = dot(in_ref[...], norm_rows(middle))
        up = t[:hidden]
        units = (up * sigmoid(up) * t[hidden:]).astype(jnp.bfloat16)
        result = middle + dot(down_ref[...], units)
        for q in range(2):
            for s in range(QUARTER):
                c = QUARTER * q + s
                rows = result[:, c * ROWS : (c + 1) * ROWS].T.reshape(2, 4, 16, CH).transpose(1, 0, 2, 3)
                held.at[h][pl.ds(c, ROWS, stride=HALF), :] = rows.reshape(ROWS, CH)
            copy = pltpu.make_async_copy(
                held.at[h].reshape(ROWS, HALF, CH).at[:, pl.ds(QUARTER * q, QUARTER), :],
                out_hbm.at[:, pl.ds(HALF * h + QUARTER * q, QUARTER), :],
                sems.at[2 * h + q],
            )
            copy.start()
            copies.append(copy)
    for copy in copies:
        copy.wait()


VMEM = pl.BlockSpec(memory_space=pltpu.VMEM)
HBM = pl.BlockSpec(memory_space=pltpu.HBM)
HELD = pltpu.VMEM((2, ROWS * HALF, CH), jnp.float32)


def call(kernel, ins, outs, scratch=(), flops=0, moved=0, out_specs=None):
    many = isinstance(outs, tuple)
    return pl.pallas_call(
        kernel,
        out_shape=outs,
        in_specs=ins,
        out_specs=out_specs if out_specs is not None else ((VMEM,) * len(outs) if many else VMEM),
        scratch_shapes=list(scratch),
        compiler_params=pltpu.CompilerParams(vmem_limit_bytes=LIMIT),
        cost_estimate=pl.CostEstimate(flops=flops, bytes_accessed=moved, transcendentals=0),
    )


def per_device(pair_rep, pair_proj, gate_proj, out_proj, trans_in, trans_out):
    bf16 = functools.partial(jax.ShapeDtypeStruct, dtype=jnp.bfloat16)
    f32 = functools.partial(jax.ShapeDtypeStruct, dtype=jnp.float32)
    flat = pair_rep.reshape(ROWS * COLS, CH)
    with jax.named_scope("norm"):
        normed = call(norm_kernel, [VMEM], bf16((2, CH, HALF * ROWS)), (), 2_000_000, 2 << 20)(flat)
    with jax.named_scope("project"):
        sides = call(
            project_kernel,
            [VMEM, VMEM],
            bf16((2, CH // 2, 2 * COLS, ROWS)),
            [pltpu.VMEM((CH * SIDES, ROWS), jnp.float32)],
            270_000_000,
            2 << 20,
        )(normed, pair_proj)
    with jax.named_scope("to_channels"):
        sides = lax.all_to_all(sides.reshape(CH, 2 * COLS, ROWS), PLANE, 0, 0, tiled=True)
    flat, sides = lax.optimization_barrier((flat, sides))
    with jax.named_scope("right_across_x"):
        right_x = lax.ppermute(sides[:, :HALF].reshape(64, COLS, ROWS), SHARE, [(d, d ^ 6) for d in range(8)])
    with jax.named_scope("right_across_x_and_core"):
        right_xc = lax.ppermute(sides[:, HALF:COLS].reshape(64, COLS, ROWS), SHARE, [(d, d ^ 7) for d in range(8)])
    with jax.named_scope("gate"):
        turn = f32((2, CH, HALF * ROWS))
        gate = call(
            gate_kernel,
            [VMEM] * 5,
            (turn, turn, bf16(out_proj.shape[::-1]), bf16(trans_in.shape[::-1]), bf16(trans_out.shape[::-1])),
            (),
            70_000_000,
            4 << 20,
        )(flat, gate_proj, out_proj, trans_in, trans_out)
    with jax.named_scope("triangle_own"):
        sums = f32((256, LEFT))
        pack, own = call(
            triangle_own_kernel, [VMEM], (bf16((2, 256, LEFT + 256)), sums), (), 140_000_000, 3 << 20
        )(sides)
    with jax.named_scope("pack_of_other_core"):
        other = lax.ppermute(pack, SHARE, [(d, d ^ 1) for d in range(8)])
    right_x, right_xc, pack, own, gate = lax.optimization_barrier((right_x, right_xc, pack, own, gate))
    with jax.named_scope("triangle_x"):
        across = call(triangle_x_kernel, [VMEM] * 2, sums, (), FLOPS_X, 2 << 20)(right_x, pack)
    across, other = lax.optimization_barrier((across, other))
    with jax.named_scope("triangle"):
        tri = call(triangle_kernel, [VMEM] * 4, bf16((32, 2, 2, COLS, ROWS)), (), 280_000_000, 4 << 20)(
            other, right_xc, own, across
        )
    with jax.named_scope("to_columns"):
        tri = lax.all_to_all(tri.reshape(CH, COLS, ROWS), PLANE, 0, 0, tiled=True)
    with jax.named_scope("finish"):
        xt, gating, proj_t, in_t, down_t = gate
        return call(
            finish_kernel,
            [VMEM] * 6,
            f32((ROWS, COLS, CH)),
            [pltpu.VMEM((CH, SUMS, ROWS), jnp.float32), HELD, pltpu.SemaphoreType.DMA((4,))],
            1_000_000_000,
            4 << 20,
            HBM,
        )(xt, gating, tri.reshape(2, CH // 2, COLS, ROWS), proj_t, in_t, down_t)


def solution(mesh):
    fine = Mesh(mesh.devices.reshape((2,) * len(AXES)), AXES)
    spec = P(AXES[:3], AXES[3:], None)
    return jax.shard_map(
        per_device, mesh=fine, in_specs=(spec, P(), P(), P(), P(), P()), out_specs=spec, check_vma=False
    )
```

```python
import functools
import itertools

import jax
import jax.numpy as jnp
from jax import lax
from jax.experimental import pallas as pl
from jax.experimental.pallas import tpu as pltpu
from jax.sharding import Mesh
from jax.sharding import PartitionSpec as P

AXES = ("xh", "xb", "zh", "y2", "y1", "y0", "zl1", "zl0", "core")
PLANE = ("xb", "y0", "zl0", "y1", "zl1", "y2", "zh")
SHARE = ("xh", "xb", "core")
ROWS = 128
COLS = 16
CH = 128
HALF = COLS // 2
QUARTER = HALF // 2
SIDES = 2 * COLS + 8
SUMS = COLS + 8
EPS = 1e-05
FLOPS_X = 16_000_000_000
LIMIT = 16 * 1024 * 1024
PROJECT_LIMIT = 60 * 1024 * 1024


def sigmoid(v):
    return 0.5 * jnp.tanh(0.5 * v) + 0.5


def norm_rows(v):
    centred = v - jnp.mean(v, axis=0, keepdims=True)
    spread = jnp.mean(centred * centred, axis=0, keepdims=True)
    return (centred * lax.rsqrt(spread + EPS)).astype(jnp.bfloat16)


def dot(a, b):
    return jnp.dot(a, b, preferred_element_type=jnp.float32)


def by_core(x):
    return x.reshape(4, 2, 16, CH).transpose(1, 0, 2, 3).reshape(2, 64, CH)


def half_columns(ref, h):
    return jnp.concatenate(
        [by_core(ref[pl.ds(HALF * h + s, ROWS, stride=COLS), :]).reshape(ROWS, CH).T for s in range(HALF)], axis=1
    )


def pairs(ref):
    tiles = []
    for pair in range(QUARTER):
        even, odd = (by_core(ref[pl.ds(2 * pair + s, ROWS, stride=HALF), :]) for s in range(2))
        tiles += [jnp.concatenate([even[c], odd[c]], axis=0).T for c in range(2)]
    return jnp.concatenate(tiles, axis=1)


def project_kernel(x_hbm, w_hbm, out_hbm, held, w_ref, stage, ready, sems):
    copies = [
        pltpu.make_async_copy(x_hbm.at[:, pl.ds(HALF * h, HALF), :], held.at[h].reshape(ROWS, HALF, CH), sems.at[h])
        for h in range(2)
    ]
    copies.append(pltpu.make_async_copy(w_hbm, w_ref, sems.at[2]))
    for copy in copies:
        copy.start()
    core, xh = lax.axis_index("core"), lax.axis_index("xh")
    normed = []
    for h in range(2):
        copies[h].wait()
        normed.append(norm_rows(pairs(held.at[h])))
    copies[2].wait()
    weights = w_ref[...].T
    sent = []
    for base, at in ((COLS, 0), (0, 2 * CH)):
        for h in range(2):
            p = dot(weights[at : at + 2 * CH], normed[h])
            values = sigmoid(p[:CH]) * p[CH:]
            for pair in range(QUARTER):
                for c in range(2):
                    lanes = slice((2 * pair + c) * ROWS, (2 * pair + c + 1) * ROWS)
                    stage[pl.ds(base + HALF * c + QUARTER * h + pair, CH, stride=SIDES), :] = values[:, lanes]
        for b in range(2):
            rows = stage[64 * SIDES * b : 64 * SIDES * (b + 1)].reshape(64, SIDES, ROWS)[:, base : base + COLS]
            if base == 0:
                first, second = rows[:, :HALF], rows[:, HALF:]
                own = jnp.where(core == 0, first, second)
                other = jnp.where(core == 0, second, first)
                rows = jnp.concatenate([own, other], axis=1)
            ready[b, :, base : base + COLS] = rows.astype(jnp.bfloat16)
            copy = pltpu.make_async_copy(
                ready.at[b, :, pl.ds(base, COLS), :],
                out_hbm.at[jnp.bitwise_xor(xh, b), :, pl.ds(base, COLS), :],
                sems.at[3 + len(sent)],
            )
            copy.start()
            sent.append(copy)
    for copy in sent:
        copy.wait()


def gate_kernel(x_ref, gate_ref, proj_ref, in_ref, down_ref, xt_ref, gating_ref, proj_t_ref, in_t_ref, down_t_ref):
    weights = gate_ref[...].T
    for h in range(2):
        xt = half_columns(x_ref, h)
        xt_ref[h] = xt
        gating_ref[h] = sigmoid(dot(weights, norm_rows(xt)))
    proj_t_ref[...] = proj_ref[...].T
    in_t_ref[...] = in_ref[...].T
    down_t_ref[...] = down_ref[...].T


def halves(sides):
    low = lax.broadcasted_iota(jnp.int32, (32 * HALF, ROWS), 1) < 64
    parts = ([], [])
    for zh in range(2):
        for x in range(2):
            first = sides[x, :, zh, COLS : COLS + HALF].reshape(32 * HALF, ROWS)
            second = sides[x, :, zh, COLS + HALF :].reshape(32 * HALF, ROWS)
            parts[0].append(jnp.where(low, first, pltpu.roll(second, 64, 1)))
            parts[1].append(jnp.where(low, pltpu.roll(first, 64, 1), second))
    return [jnp.concatenate(part, axis=1).astype(jnp.bfloat16) for part in parts]


def turned(right):
    blocks = [right[x, :, zh].reshape(32 * HALF, ROWS).astype(jnp.bfloat16).T for x in range(2) for zh in range(2)]
    return [
        jnp.concatenate([block[64 * s : 64 * s + 64] for block in blocks], axis=0) for s in range(2)
    ]


def product(right, left):
    return dot(right[0], left[0]) + dot(right[1], left[1])


def wide(ref, rows):
    return ref[...].astype(jnp.float32).reshape(2, 32, 2, rows, ROWS)


LEFT = 4 * ROWS


def triangle_own_kernel(sides_ref, pack_ref, own_ref):
    sides = wide(sides_ref, 2 * COLS)
    left, right = halves(sides), turned(sides[:, :, :, HALF:COLS])
    for s in range(2):
        pack_ref[s, :, :LEFT] = left[s]
        pack_ref[s, :, LEFT:] = right[s]
    own_ref[...] = product(turned(sides[:, :, :, :HALF]), left)


def triangle_x_kernel(x_ref, pack_ref, across_ref):
    across_ref[...] = product(turned(wide(x_ref, HALF)), [pack_ref[s, :, :LEFT] for s in range(2)])


def triangle_kernel(other_ref, xc_ref, own_ref, across_ref, out_ref):
    xh = lax.axis_index("xh")
    left = [other_ref[s, :, :LEFT] for s in range(2)]
    own = own_ref[...] + product([other_ref[s, :, LEFT:] for s in range(2)], left)
    across = across_ref[...] + product(turned(wide(xc_ref, HALF)), left)
    for total, at in ((own, xh), (across, 1 - xh)):
        total = total.astype(jnp.bfloat16).reshape(2, 2, 4, 16, 4 * ROWS)
        for x, zj, z0, xj, z1, zh in itertools.product(range(2), repeat=6):
            lanes = slice((2 * zh + x) * ROWS, (2 * zh + x + 1) * ROWS)
            out_ref[16 * x + 8 * zj + 4 * z0 + 2 * xj + z1, at, zh] = total[xj, zj, 2 * z1 + z0, :, lanes]


def finish_kernel(xt_ref, gating_ref, t_ref, proj_ref, in_ref, down_ref, out_hbm, stage, held, sems):
    xh = lax.axis_index("xh")
    for b in range(2):
        stage[64 * b : 64 * b + 64, :COLS] = t_ref[jnp.bitwise_xor(xh, b)].astype(jnp.float32)
    sums = stage.reshape(CH * SUMS, ROWS)
    hidden = down_ref.shape[1]
    copies = []
    for h in range(2):
        tri = jnp.concatenate([sums[pl.ds(HALF * h + s, CH, stride=SUMS), :] for s in range(HALF)], axis=1)
        middle = xt_ref[h] + gating_ref[h] * dot(proj_ref[...], norm_rows(tri))
        t = dot(in_ref[...], norm_rows(middle))
        up = t[:hidden]
        units = (up * sigmoid(up) * t[hidden:]).astype(jnp.bfloat16)
        result = middle + dot(down_ref[...], units)
        for q in range(2):
            for s in range(QUARTER):
                c = QUARTER * q + s
                rows = result[:, c * ROWS : (c + 1) * ROWS].T.reshape(2, 4, 16, CH).transpose(1, 0, 2, 3)
                held.at[h][pl.ds(c, ROWS, stride=HALF), :] = rows.reshape(ROWS, CH)
            copy = pltpu.make_async_copy(
                held.at[h].reshape(ROWS, HALF, CH).at[:, pl.ds(QUARTER * q, QUARTER), :],
                out_hbm.at[:, pl.ds(HALF * h + QUARTER * q, QUARTER), :],
                sems.at[2 * h + q],
            )
            copy.start()
            copies.append(copy)
    for copy in copies:
        copy.wait()


VMEM = pl.BlockSpec(memory_space=pltpu.VMEM)
HBM = pl.BlockSpec(memory_space=pltpu.HBM)
HELD = pltpu.VMEM((2, ROWS * HALF, CH), jnp.float32)


def call(kernel, ins, outs, scratch=(), flops=0, moved=0, out_specs=None, limit=LIMIT):
    many = isinstance(outs, tuple)
    return pl.pallas_call(
        kernel,
        out_shape=outs,
        in_specs=ins,
        out_specs=out_specs if out_specs is not None else ((VMEM,) * len(outs) if many else VMEM),
        scratch_shapes=list(scratch),
        compiler_params=pltpu.CompilerParams(vmem_limit_bytes=limit),
        cost_estimate=pl.CostEstimate(flops=flops, bytes_accessed=moved, transcendentals=0),
    )


def per_device(pair_rep, pair_proj, gate_proj, out_proj, trans_in, trans_out):
    bf16 = functools.partial(jax.ShapeDtypeStruct, dtype=jnp.bfloat16)
    f32 = functools.partial(jax.ShapeDtypeStruct, dtype=jnp.float32)
    flat = pair_rep.reshape(ROWS * COLS, CH)
    with jax.named_scope("project"):
        sides = call(
            project_kernel,
            [HBM, HBM],
            bf16((2, CH // 2, 2 * COLS, ROWS)),
            [
                HELD,
                pltpu.VMEM(pair_proj.shape, jnp.bfloat16),
                pltpu.VMEM((CH * SIDES, ROWS), jnp.float32),
                pltpu.VMEM((2, CH // 2, 2 * COLS, ROWS), jnp.bfloat16),
                pltpu.SemaphoreType.DMA((7,)),
            ],
            270_000_000,
            2 << 20,
            HBM,
            PROJECT_LIMIT,
        )(pair_rep, pair_proj)
    with jax.named_scope("to_channels"):
        sides = lax.all_to_all(sides.reshape(CH, 2 * COLS, ROWS), PLANE, 0, 0, tiled=True)
    flat, sides = lax.optimization_barrier((flat, sides))
    with jax.named_scope("right_across_x"):
        right_x = lax.ppermute(sides[:, :HALF].reshape(64, COLS, ROWS), SHARE, [(d, d ^ 6) for d in range(8)])
    with jax.named_scope("right_across_x_and_core"):
        right_xc = lax.ppermute(sides[:, HALF:COLS].reshape(64, COLS, ROWS), SHARE, [(d, d ^ 7) for d in range(8)])
    with jax.named_scope("gate"):
        turn = f32((2, CH, HALF * ROWS))
        gate = call(
            gate_kernel,
            [VMEM] * 5,
            (turn, turn, bf16(out_proj.shape[::-1]), bf16(trans_in.shape[::-1]), bf16(trans_out.shape[::-1])),
            (),
            70_000_000,
            4 << 20,
        )(flat, gate_proj, out_proj, trans_in, trans_out)
    with jax.named_scope("triangle_own"):
        sums = f32((256, LEFT))
        pack, own = call(
            triangle_own_kernel, [VMEM], (bf16((2, 256, LEFT + 256)), sums), (), 140_000_000, 3 << 20
        )(sides)
    with jax.named_scope("pack_of_other_core"):
        other = lax.ppermute(pack, SHARE, [(d, d ^ 1) for d in range(8)])
    right_x, right_xc, pack, own, gate = lax.optimization_barrier((right_x, right_xc, pack, own, gate))
    with jax.named_scope("triangle_x"):
        across = call(triangle_x_kernel, [VMEM] * 2, sums, (), FLOPS_X, 2 << 20)(right_x, pack)
    across, other = lax.optimization_barrier((across, other))
    with jax.named_scope("triangle"):
        tri = call(triangle_kernel, [VMEM] * 4, bf16((32, 2, 2, COLS, ROWS)), (), 280_000_000, 4 << 20)(
            other, right_xc, own, across
        )
    with jax.named_scope("to_columns"):
        tri = lax.all_to_all(tri.reshape(CH, COLS, ROWS), PLANE, 0, 0, tiled=True)
    with jax.named_scope("finish"):
        xt, gating, proj_t, in_t, down_t = gate
        return call(
            finish_kernel,
            [VMEM] * 6,
            f32((ROWS, COLS, CH)),
            [pltpu.VMEM((CH, SUMS, ROWS), jnp.float32), HELD, pltpu.SemaphoreType.DMA((4,))],
            1_000_000_000,
            4 << 20,
            HBM,
        )(xt, gating, tri.reshape(2, CH // 2, COLS, ROWS), proj_t, in_t, down_t)


def solution(mesh):
    fine = Mesh(mesh.devices.reshape((2,) * len(AXES)), AXES)
    spec = P(AXES[:3], AXES[3:], None)
    return jax.shard_map(
        per_device, mesh=fine, in_specs=(spec, P(), P(), P(), P(), P()), out_specs=spec, check_vma=False
    )
```

```python
import functools
import itertools

import jax
import jax.numpy as jnp
from jax import lax
from jax.experimental import pallas as pl
from jax.experimental.pallas import tpu as pltpu
from jax.sharding import Mesh
from jax.sharding import PartitionSpec as P

AXES = ("xh", "xb", "zh", "y2", "y1", "y0", "zl1", "zl0", "core")
PLANE = ("xb", "y0", "zl0", "y1", "zl1", "y2", "zh")
SHARE = ("xh", "xb", "core")
ROWS = 128
COLS = 16
CH = 128
HALF = COLS // 2
QUARTER = HALF // 2
SIDES = 2 * COLS + 8
SUMS = COLS + 8
EPS = 1e-05
FLOPS_X = 16_000_000_000
LIMIT = 16 * 1024 * 1024


def sigmoid(v):
    return 0.5 * jnp.tanh(0.5 * v) + 0.5


def norm_rows(v):
    centred = v - jnp.mean(v, axis=0, keepdims=True)
    spread = jnp.mean(centred * centred, axis=0, keepdims=True)
    return (centred * lax.rsqrt(spread + EPS)).astype(jnp.bfloat16)


def dot(a, b):
    return jnp.dot(a, b, preferred_element_type=jnp.float32)


def by_core(x):
    return x.reshape(4, 2, 16, CH).transpose(1, 0, 2, 3).reshape(2, 64, CH)


def half_columns(ref, h):
    return jnp.concatenate(
        [by_core(ref[pl.ds(HALF * h + s, ROWS, stride=COLS), :]).reshape(ROWS, CH).T for s in range(HALF)], axis=1
    )


def half_pairs(ref, h):
    tiles = []
    for pair in range(QUARTER):
        even, odd = (by_core(ref[pl.ds(HALF * h + 2 * pair + s, ROWS, stride=COLS), :]) for s in range(2))
        tiles += [jnp.concatenate([even[c], odd[c]], axis=0).T for c in range(2)]
    return jnp.concatenate(tiles, axis=1)


def norm_kernel(x_ref, normed_ref):
    for h in range(2):
        normed_ref[h] = norm_rows(half_pairs(x_ref, h))


def project_kernel(normed_ref, w_ref, out_ref, stage):
    core = lax.axis_index("core")
    weights = w_ref[...].T
    for h in range(2):
        p = dot(weights, normed_ref[h])
        left = sigmoid(p[:CH]) * p[CH : 2 * CH]
        right = sigmoid(p[2 * CH : 3 * CH]) * p[3 * CH :]
        for pair in range(QUARTER):
            row = QUARTER * h + pair
            for c in range(2):
                at = slice((2 * pair + c) * ROWS, (2 * pair + c + 1) * ROWS)
                stage[pl.ds(HALF * c + row, CH, stride=SIDES), :] = right[:, at]
                stage[pl.ds(COLS + HALF * c + row, CH, stride=SIDES), :] = left[:, at]
    xh = lax.axis_index("xh")
    for b in range(2):
        rows = stage[64 * SIDES * b : 64 * SIDES * (b + 1)].reshape(64, SIDES, ROWS)
        first, second = rows[:, :HALF], rows[:, HALF:COLS]
        own = jnp.where(core == 0, first, second)
        other = jnp.where(core == 0, second, first)
        rows = jnp.concatenate([own, other, rows[:, COLS : 2 * COLS]], axis=1)
        out_ref[jnp.bitwise_xor(xh, b)] = rows.astype(jnp.bfloat16)


def gate_kernel(x_ref, gate_ref, proj_ref, in_ref, down_ref, xt_ref, gating_ref, proj_t_ref, in_t_ref, down_t_ref):
    weights = gate_ref[...].T
    for h in range(2):
        xt = half_columns(x_ref, h)
        xt_ref[h] = xt
        gating_ref[h] = sigmoid(dot(weights, norm_rows(xt)))
    proj_t_ref[...] = proj_ref[...].T
    in_t_ref[...] = in_ref[...].T
    down_t_ref[...] = down_ref[...].T


def halves(sides):
    low = lax.broadcasted_iota(jnp.int32, (32 * HALF, ROWS), 1) < 64
    parts = ([], [])
    for zh in range(2):
        for x in range(2):
            first = sides[x, :, zh, COLS : COLS + HALF].reshape(32 * HALF, ROWS)
            second = sides[x, :, zh, COLS + HALF :].reshape(32 * HALF, ROWS)
            parts[0].append(jnp.where(low, first, pltpu.roll(second, 64, 1)))
            parts[1].append(jnp.where(low, pltpu.roll(first, 64, 1), second))
    return [jnp.concatenate(part, axis=1).astype(jnp.bfloat16) for part in parts]


def turned(right):
    blocks = [right[x, :, zh].reshape(32 * HALF, ROWS).astype(jnp.bfloat16).T for x in range(2) for zh in range(2)]
    return [
        jnp.concatenate([block[64 * s : 64 * s + 64] for block in blocks], axis=0) for s in range(2)
    ]


def product(right, left):
    return dot(right[0], left[0]) + dot(right[1], left[1])


def wide(ref, rows):
    return ref[...].astype(jnp.float32).reshape(2, 32, 2, rows, ROWS)


LEFT = 4 * ROWS


def triangle_own_kernel(sides_ref, pack_ref, own_ref):
    sides = wide(sides_ref, 2 * COLS)
    left, right = halves(sides), turned(sides[:, :, :, HALF:COLS])
    for s in range(2):
        pack_ref[s, :, :LEFT] = left[s]
        pack_ref[s, :, LEFT:] = right[s]
    own_ref[...] = product(turned(sides[:, :, :, :HALF]), left)


def triangle_x_kernel(x_ref, pack_ref, across_ref):
    across_ref[...] = product(turned(wide(x_ref, HALF)), [pack_ref[s, :, :LEFT] for s in range(2)])


def triangle_kernel(other_ref, xc_ref, own_ref, across_ref, out_ref):
    xh = lax.axis_index("xh")
    left = [other_ref[s, :, :LEFT] for s in range(2)]
    own = own_ref[...] + product([other_ref[s, :, LEFT:] for s in range(2)], left)
    across = across_ref[...] + product(turned(wide(xc_ref, HALF)), left)
    for total, at in ((own, xh), (across, 1 - xh)):
        total = total.astype(jnp.bfloat16).reshape(2, 2, 4, 16, 4 * ROWS)
        for x, zj, z0, xj, z1, zh in itertools.product(range(2), repeat=6):
            lanes = slice((2 * zh + x) * ROWS, (2 * zh + x + 1) * ROWS)
            out_ref[16 * x + 8 * zj + 4 * z0 + 2 * xj + z1, at, zh] = total[xj, zj, 2 * z1 + z0, :, lanes]


def finish_kernel(xt_ref, gating_ref, t_ref, proj_ref, in_ref, down_ref, out_hbm, stage, held, sems):
    xh = lax.axis_index("xh")
    for b in range(2):
        stage[64 * b : 64 * b + 64, :COLS] = t_ref[jnp.bitwise_xor(xh, b)].astype(jnp.float32)
    sums = stage.reshape(CH * SUMS, ROWS)
    hidden = down_ref.shape[1]
    copies = []
    for h in range(2):
        tri = jnp.concatenate([sums[pl.ds(HALF * h + s, CH, stride=SUMS), :] for s in range(HALF)], axis=1)
        middle = xt_ref[h] + gating_ref[h] * dot(proj_ref[...], norm_rows(tri))
        t = dot(in_ref[...], norm_rows(middle))
        up = t[:hidden]
        units = (up * sigmoid(up) * t[hidden:]).astype(jnp.bfloat16)
        result = middle + dot(down_ref[...], units)
        for c in range(HALF):
            rows = result[:, c * ROWS : (c + 1) * ROWS].T.reshape(2, 4, 16, CH).transpose(1, 0, 2, 3)
            held.at[h][pl.ds(c, ROWS, stride=HALF), :] = rows.reshape(ROWS, CH)
        copy = pltpu.make_async_copy(
            held.at[h].reshape(ROWS, HALF, CH), out_hbm.at[:, pl.ds(HALF * h, HALF), :], sems.at[h]
        )
        copy.start()
        copies.append(copy)
    for copy in copies:
        copy.wait()


VMEM = pl.BlockSpec(memory_space=pltpu.VMEM)
HBM = pl.BlockSpec(memory_space=pltpu.HBM)
HELD = pltpu.VMEM((2, ROWS * HALF, CH), jnp.float32)


def call(kernel, ins, outs, scratch=(), flops=0, moved=0, out_specs=None):
    many = isinstance(outs, tuple)
    return pl.pallas_call(
        kernel,
        out_shape=outs,
        in_specs=ins,
        out_specs=out_specs if out_specs is not None else ((VMEM,) * len(outs) if many else VMEM),
        scratch_shapes=list(scratch),
        compiler_params=pltpu.CompilerParams(vmem_limit_bytes=LIMIT),
        cost_estimate=pl.CostEstimate(flops=flops, bytes_accessed=moved, transcendentals=0),
    )


def per_device(pair_rep, pair_proj, gate_proj, out_proj, trans_in, trans_out):
    bf16 = functools.partial(jax.ShapeDtypeStruct, dtype=jnp.bfloat16)
    f32 = functools.partial(jax.ShapeDtypeStruct, dtype=jnp.float32)
    flat = pair_rep.reshape(ROWS * COLS, CH)
    with jax.named_scope("norm"):
        normed = call(norm_kernel, [VMEM], bf16((2, CH, HALF * ROWS)), (), 2_000_000, 2 << 20)(flat)
    with jax.named_scope("project"):
        sides = call(
            project_kernel,
            [VMEM, VMEM],
            bf16((2, CH // 2, 2 * COLS, ROWS)),
            [pltpu.VMEM((CH * SIDES, ROWS), jnp.float32)],
            270_000_000,
            2 << 20,
        )(normed, pair_proj)
    with jax.named_scope("to_channels"):
        sides = lax.all_to_all(sides.reshape(CH, 2 * COLS, ROWS), PLANE, 0, 0, tiled=True)
    flat, sides = lax.optimization_barrier((flat, sides))
    with jax.named_scope("right_across_x"):
        right_x = lax.ppermute(sides[:, :HALF].reshape(64, COLS, ROWS), SHARE, [(d, d ^ 6) for d in range(8)])
    with jax.named_scope("right_across_x_and_core"):
        right_xc = lax.ppermute(sides[:, HALF:COLS].reshape(64, COLS, ROWS), SHARE, [(d, d ^ 7) for d in range(8)])
    with jax.named_scope("gate"):
        turn = f32((2, CH, HALF * ROWS))
        gate = call(
            gate_kernel,
            [VMEM] * 5,
            (turn, turn, bf16(out_proj.shape[::-1]), bf16(trans_in.shape[::-1]), bf16(trans_out.shape[::-1])),
            (),
            70_000_000,
            4 << 20,
        )(flat, gate_proj, out_proj, trans_in, trans_out)
    with jax.named_scope("triangle_own"):
        sums = f32((256, LEFT))
        pack, own = call(
            triangle_own_kernel, [VMEM], (bf16((2, 256, LEFT + 256)), sums), (), 140_000_000, 3 << 20
        )(sides)
    with jax.named_scope("pack_of_other_core"):
        other = lax.ppermute(pack, SHARE, [(d, d ^ 1) for d in range(8)])
    right_x, right_xc, pack, own, gate = lax.optimization_barrier((right_x, right_xc, pack, own, gate))
    with jax.named_scope("triangle_x"):
        across = call(triangle_x_kernel, [VMEM] * 2, sums, (), FLOPS_X, 2 << 20)(right_x, pack)
    across, other = lax.optimization_barrier((across, other))
    with jax.named_scope("triangle"):
        tri = call(triangle_kernel, [VMEM] * 4, bf16((32, 2, 2, COLS, ROWS)), (), 280_000_000, 4 << 20)(
            other, right_xc, own, across
        )
    with jax.named_scope("to_columns"):
        tri = lax.all_to_all(tri.reshape(CH, COLS, ROWS), PLANE, 0, 0, tiled=True)
    with jax.named_scope("finish"):
        xt, gating, proj_t, in_t, down_t = gate
        return call(
            finish_kernel,
            [VMEM] * 6,
            f32((ROWS, COLS, CH)),
            [pltpu.VMEM((CH, SUMS, ROWS), jnp.float32), HELD, pltpu.SemaphoreType.DMA((2,))],
            1_000_000_000,
            4 << 20,
            HBM,
        )(xt, gating, tri.reshape(2, CH // 2, COLS, ROWS), proj_t, in_t, down_t)


def solution(mesh):
    fine = Mesh(mesh.devices.reshape((2,) * len(AXES)), AXES)
    spec = P(AXES[:3], AXES[3:], None)
    return jax.shard_map(
        per_device, mesh=fine, in_specs=(spec, P(), P(), P(), P(), P()), out_specs=spec, check_vma=False
    )
```
